32 devices in a mesh: group: 2 (over y), tm: 4 (over x, core), space: 4 (over z).
Axes of the slice: x: 2, y: 2, z: 4, core: 2. Of those that a mesh axis runs over, the one named last changes fastest.
Arguments:
- start_latent: float32 [32, 32, 256], P('group', 'space'), parts along dimension 0, may hold values from -6 to 6
- time_embed: float32 [8, 128], P('tm'), may hold values from -6 to 6
- drift_x: float32 [8], P('tm'), may hold values from -0.06 to -0.01
- drift_eps: float32 [8], P('tm'), may hold values from 0.02 to 0.1
- w_in: float32 [3, 3, 128, 16], replicated, may hold values from -0.5 to 0.5
- b_in: float32 [128], replicated, may hold values from -3 to 3
- w_mid: float32 [3, 3, 128, 128], replicated, may hold values from -0.1875 to 0.1875
- b_mid: float32 [128], replicated, may hold values from -3 to 3
- w_out: float32 [3, 3, 16, 128], replicated, may hold values from -0.1875 to 0.1875
- b_out: float32 [16], replicated, may hold values from -3 to 3
Outputs:
- trajectory: float32 [8, 32, 32, 256], P('tm', 'group', 'space'), parts along dimension 1
The draws below stay inside these ranges and needn't reach their ends.
There are 2 independent parts, one for each index of `group`. The reference program is written for one: setup_inputs(seed, part) draws one part's arguments, and reference() takes and returns one part's arrays. A program takes and returns all parts, laid end to end along the dimension named above; an argument that names none is the same for every part. Nothing has to cross between parts.
All inputs are finite; a program needn't handle non-finite values.
Results may differ from the reference program's by a relative error of at most 0.0001.
Values sent between devices are 32-bit elements; how exact they have to be, the bound alone decides.
No kernel may reach another device: no remote copies, remote signals or barrier semaphores. Data moves between devices by JAX's collectives and lax.ppermute only.
A program may use at most 64 MiB of HBM per device.

```python
import math
import jax
import jax.numpy as jnp
from jax import lax

C = 16
HID = 128
COLS = 256
ITERS = 2
STATES = 8
HEIGHT = 32


def block_levels(stream_key, shape, split, smallest, top_value):
    def one(dim, blocks):
        heights = jax.random.uniform(jax.random.fold_in(jax.random.fold_in(stream_key, 6), dim), (blocks,), jnp.float32, smallest / len(split), top_value / len(split))
        return jnp.repeat(jnp.exp(heights), shape[dim] // blocks).reshape((-1,) + (1,) * (len(shape) - dim - 1))

    level = one(*split[0])
    for cut in split[1:]:
        level = level * one(*cut)
    return level


def bell_draw(rng, shape, scale, limit, cuts=(), held_as=jnp.bfloat16):
    loudness = block_levels(rng, shape, cuts, -0.22, 0.18) if cuts else 1.0
    array = jax.random.normal(rng, shape, jnp.float32) * scale * loudness
    return jnp.minimum(jnp.maximum(array, -limit), limit).astype(held_as)


def setup_inputs(seed: int = 0, part: int = 0) -> dict:
    key_list = jax.random.split(jax.random.key(seed), 11)
    own_keys = jax.random.split(jax.random.fold_in(key_list[10], part), 11)
    return {
        "start_latent": bell_draw(own_keys[0], (C, HEIGHT, COLS), 1.0, 6.0, ((1, 4),), jnp.float32),
        "time_embed": bell_draw(key_list[1], (STATES, HID), 1.0, 6.0, ((0, 4),), jnp.float32),
        "drift_x": jnp.clip(-0.06 + 0.04999999888241291 * jax.random.uniform(key_list[2], (STATES,), jnp.float32) ** block_levels(key_list[2], (STATES,), ((0, 4),), -0.2, 0.2), -0.06, -0.01),
        "drift_eps": jnp.clip(jnp.exp(math.log(0.1) - 1.609438 * jax.random.uniform(key_list[3], (STATES,), jnp.float32) ** block_levels(key_list[3], (STATES,), ((0, 4),), -0.2, 0.2)), 0.02, 0.1),
        "w_in": bell_draw(key_list[4], (3, 3, HID, C), (9 * C) ** -0.5, 0.5, (), jnp.float32),
        "b_in": bell_draw(key_list[5], (HID,), 0.5, 3.0, (), jnp.float32),
        "w_mid": bell_draw(key_list[6], (3, 3, HID, HID), (9 * HID) ** -0.5, 0.1875, (), jnp.float32),
        "b_mid": bell_draw(key_list[7], (HID,), 0.5, 3.0, (), jnp.float32),
        "w_out": bell_draw(key_list[8], (3, 3, C, HID), (9 * HID) ** -0.5, 0.1875, (), jnp.float32),
        "b_out": bell_draw(key_list[9], (C,), 0.5, 3.0, (), jnp.float32),
    }


def convolve(field, weight):
    kernel = jnp.transpose(weight, (2, 3, 0, 1))
    result = lax.conv_general_dilated(field[None], kernel, (1, 1), ((1, 1), (1, 1)), dimension_numbers=("NCHW", "OIHW", "NCHW"), precision=lax.Precision.HIGHEST)
    return result[0]


def reference(start_latent, time_embed, drift_x, drift_eps, w_in, b_in, w_mid, b_mid, w_out, b_out):
    def denoise_state(operands):
        field, embedding = operands
        first_hidden = jax.nn.silu(convolve(field, w_in) + (b_in + embedding)[:, None, None])
        second_hidden = jax.nn.silu(convolve(first_hidden, w_mid) + b_mid[:, None, None])
        return convolve(second_hidden, w_out) + b_out[:, None, None]

    trajectory = jnp.broadcast_to(start_latent[None], (STATES,) + start_latent.shape)
    for iteration in range(ITERS):
        inputs = jnp.concatenate([start_latent[None], trajectory[:-1]], 0)
        noise_pred = lax.map(denoise_state, (inputs, time_embed))
        drift = drift_x[:, None, None, None] * inputs + drift_eps[:, None, None, None] * noise_pred
        trajectory = start_latent[None] + jnp.cumsum(drift, 0)
    return trajectory
```

```python
import functools
import jax
import jax.numpy as jnp
from jax import lax
from jax.experimental import pallas as pl
from jax.experimental.pallas import tpu as pltpu
from jax.sharding import PartitionSpec as P

REACH = 3
HALO = 2 * REACH
OFF = -1e30
VMEM_LIMIT = 56 * 2**20
F32, BF16 = jnp.float32, jnp.bfloat16


def split(value):
    high = value.astype(BF16)
    return high, (value - high.astype(F32)).astype(BF16)


def silu(value):
    half = 0.5 * value
    return half + half * jnp.tanh(half)


def lane_groups(shape, size):
    return lax.broadcasted_iota(jnp.int32, shape, len(shape) - 1) // size


def weights_kernel(wi_ref, wm_ref, wo_ref, wi_out, wm_out, wo_out):
    depth = wi_ref.shape[0]
    high, low = split(wi_ref[...])
    rest = jnp.zeros((wi_out.shape[0] - 3 * depth, wi_ref.shape[1]), BF16)
    wi_out[...] = jnp.concatenate([high, high, low, rest], 0)
    hid = wm_ref.shape[-1]
    for a in range(3):
        w0, w1, w2 = (wm_ref[a, b].T for b in range(3))
        even, odd = w0 * (1 / 24) + w2 * (1 / 6), w1 * (1 / 12)
        sides = (w0 + w2) * (-1 / 6)
        middle = w1 * (-1 / 6)
        forms = (w0 * 0.25, sides + middle, sides - middle, even + odd, even - odd, w2)
        for point, form in enumerate(forms):
            both = jnp.concatenate(split(form), 1)
            wm_out[point, 2 * a * hid : (2 * a + 1) * hid] = both
            wm_out[point, (2 * a + 1) * hid : (2 * a + 2) * hid] = both
        out = wo_ref[a]
        high = out.astype(BF16).astype(F32)
        third = lane_groups(out.shape, out.shape[-1] // 8) < 3
        both = jnp.where(third, high, out - high).astype(BF16)
        wo_out[2 * a * hid : (2 * a + 1) * hid] = both
        wo_out[(2 * a + 1) * hid : (2 * a + 2) * hid] = both


def main_kernel(
    tm, up_ref, mid_ref, down_ref, par_ref, bias_ref, wi_ref, wm_ref, wo_ref, *refs
):
    outs = refs[:tm]
    start_s, points_s, hid2_s, inputs_s, packed_s, chunk_s, in_bias, mid_bias, eps_s = refs[tm:]
    rows, chans = mid_ref.shape[0], mid_ref.shape[1]
    states, hid = par_ref.shape[0], wm_ref.shape[2] // 2
    groups = points_s.shape[2] // states
    wide = 4 * groups
    cols = wide - 8
    my_tm, my_space = lax.axis_index("tm"), lax.axis_index("space")
    all_rows, all_cols = rows * lax.axis_size("space"), cols * tm
    row0, col0 = my_space * rows, my_tm * cols
    replicas = hid // chans

    embed, drift_x, drift_eps = par_ref[:, :hid], par_ref[:, hid : hid + 1], par_ref[:, hid + 1 : hid + 2]
    drift_x = jnp.broadcast_to(drift_x, (states, hid))

    def inside(first, width, limit):
        place = lax.broadcasted_iota(jnp.int32, (width, states, hid), 0)
        return (place + first >= 0) & (place + first < all_cols) & (place < limit)

    bias = bias_ref[0:1] + embed
    in_bias[0] = jnp.full(in_bias.shape[1:], OFF, F32)
    in_bias[1] = jnp.where(inside(col0 - 5, wide + 4, wide + 2), bias[None], OFF)
    mid_bias[0] = jnp.full(mid_bias.shape[1:], OFF, F32)
    mid_bias[1] = jnp.where(
        inside(col0 - 4, mid_bias.shape[1], mid_bias.shape[1]),
        jnp.broadcast_to(bias_ref[1:2], (states, hid))[None],
        OFF,
    )
    eps_s[0] = jnp.zeros(eps_s.shape[1:], F32)
    eps_s[1] = jnp.where(
        inside(col0 - 3, wide, wide), jnp.broadcast_to(drift_eps, (states, hid))[None], 0.0
    )
    out_bias = bias_ref[2:3]

    def in_field(row):
        return jnp.where((row >= 0) & (row < all_rows), 1, 0)

    for ref, first in ((up_ref, 0), (mid_ref, HALO), (down_ref, HALO + rows)):

        def turn(i, _, ref=ref, first=first):
            start_s[first + i] = jnp.concatenate([ref[i]] * replicas, 0).T
            return 0

        lax.fori_loop(0, ref.shape[0], turn, 0)

    def stacked(r0, r1, r2):
        place = lane_groups(r0.shape, chans)
        value = jnp.where(place % 3 == 0, r0, jnp.where(place % 3 == 1, r1, r2))
        high = value.astype(BF16).astype(F32)
        low_part = (place >= 3) & (place < 6)
        return jnp.concatenate(
            [jnp.where(low_part, value - high, value).astype(BF16), r2.astype(BF16)], 1
        )

    def first_conv(left):
        return jnp.dot(left, wi_ref[...], preferred_element_type=F32)

    def to_points(row, field):
        fours = field.reshape(groups + 1, 4, states, hid)
        d0, d1, d2, d3 = (fours[:groups, k] for k in range(4))
        d4, d5 = fours[1:, 0], fours[1:, 1]
        e1, e2 = d4 - 4 * d2, d3 - 4 * d1
        e3, e4 = d4 - d2, 2 * (d3 - d1)
        forms = (4 * d0 - 5 * d2 + d4, e1 + e2, e1 - e2, e3 + e4, e3 - e4, 4 * d1 - 5 * d3 + d5)
        for point, form in enumerate(forms):
            high, low = split(form.reshape(groups * states, hid))
            points_s[point, row, :, :hid] = high
            points_s[point, row, :, hid:] = low

    def second_hidden(count, step, row_first, col_first):
        def body(c, _):
            first = c * step
            sums = []
            for point in range(6):
                left = jnp.concatenate(
                    [
                        points_s[point, pl.ds(first + a, step)].reshape(step * groups * states, 2 * hid)
                        for a in range(3)
                    ],
                    1,
                )
                both = jnp.dot(left, wm_ref[point], preferred_element_type=F32)
                sums.append((both[:, :hid] + both[:, hid:]).reshape(step, groups, states, hid))
            m0, m1, m2, m3, m4, m5 = sums
            s1, t1, s3, t3 = m1 + m2, m1 - m2, m3 + m4, m3 - m4
            field = jnp.stack(
                [m0 + s1 + s3, t1 + 2 * t3, s1 + 4 * s3, t1 + 8 * t3 + m5], 2
            ).reshape(step, wide, states, hid)
            for r in range(step):
                ok = in_field(row0 + row_first + first + r)
                value = silu(field[r] + mid_bias[ok, col_first : col_first + wide])
                high, low = split(value.reshape(wide * states, hid))
                hid2_s[first + r, :, :hid] = high
                hid2_s[first + r, :, hid:] = low
            return 0

        lax.fori_loop(0, count // step, body, 0)

    def noise(first, step, width):
        left = jnp.concatenate(
            [
                hid2_s[pl.ds(first + a, step)].reshape(step * wide * states, 2 * hid)
                for a in range(3)
            ],
            1,
        )
        taps = jnp.dot(left, wo_ref[...], preferred_element_type=F32)
        taps = taps.reshape(step, wide, states, hid)
        shape = (step, width, states, hid)
        place = lane_groups(shape, chans) % 3
        value = jnp.where(
            place == 0,
            taps[:, 0:width],
            jnp.where(place == 1, taps[:, 1 : width + 1], taps[:, 2 : width + 2]),
        ).reshape(step * width * states, hid)
        size = hid // 2
        while size >= chans:
            value = value + pltpu.roll(value, size, 1)
            size //= 2
        return (value + out_bias).reshape(shape)

    state = lax.broadcasted_iota(jnp.int32, (1, states, hid), 1)

    def earlier(value):
        value = jnp.where(state >= 1, pltpu.roll(value, 1, 1), 0.0)
        reach = 1
        while reach < states:
            value = value + jnp.where(state >= reach, pltpu.roll(value, reach, 1), 0.0)
            reach *= 2
        return value

    def first_rows(i, _):
        depth = start_s.shape[1]
        left = stacked(start_s[i], start_s[i + 1], start_s[i + 2])
        taps = first_conv(left)
        t0, t1, t2 = (taps[:, k * hid : (k + 1) * hid] for k in range(3))
        common = t0 + pltpu.roll(t1, depth - 1, 0) + pltpu.roll(t2, depth - 2, 0)
        ok = in_field(row0 - 5 + i)
        to_points(i, silu(common[: wide + 4, None, :] + in_bias[ok]))
        return 0

    lax.fori_loop(0, rows + 10, first_rows, 0)
    second_hidden(rows + 8, 4 if rows % 4 == 0 else 1, -4, 0)
    reach_cols = cols + HALO

    def next_inputs(i, _):
        value = noise(i, 1, reach_cols)[0]
        ok = in_field(row0 - REACH + i)
        start = jnp.broadcast_to(
            start_s[REACH + i, REACH : REACH + reach_cols, :][:, None, :], (reach_cols, states, hid)
        )
        drift = drift_x[None] * start + eps_s[ok, :reach_cols] * value
        value = (start + earlier(drift)).reshape(reach_cols * states, hid)
        inputs_s[i, : reach_cols * states] = value
        inputs_s[i, reach_cols * states :] = jnp.zeros(((wide - reach_cols) * states, hid), F32)
        return 0

    lax.fori_loop(0, rows + HALO, next_inputs, 0)

    def second_rows(i, _):
        taps = first_conv(stacked(inputs_s[i], inputs_s[i + 1], inputs_s[i + 2]))
        width = cols + 4
        t0, t1, t2 = (
            taps[k * states : (k + width) * states, k * hid : (k + 1) * hid] for k in range(3)
        )
        ok = in_field(row0 - 2 + i)
        value = silu((t0 + t1 + t2).reshape(width, states, hid) + in_bias[ok, 3 : 3 + width])
        to_points(i, jnp.concatenate([value, jnp.zeros((8, states, hid), F32)], 0))
        return 0

    lax.fori_loop(0, rows + 4, second_rows, 0)
    second_hidden(rows + 2, 5 if (rows + 2) % 5 == 0 else 1, -1, 3)

    packed = jnp.zeros((cols * states, hid), F32)
    place = lane_groups((cols * states, hid), chans)
    packed_s[...] = packed

    def last_rows(i, _):
        value = noise(i, 1, cols)[0]
        here = inputs_s[REACH + i, REACH * states : (REACH + cols) * states]
        drift = drift_x[None] * here.reshape(cols, states, hid) + drift_eps[None] * value
        packed_s[...] = jnp.where(place == i, drift.reshape(cols * states, hid), packed_s[...])
        return 0

    lax.fori_loop(0, rows, last_rows, 0)

    size = cols * states
    source = lax.broadcasted_iota(jnp.int32, (size, size), 0)
    target = lax.broadcasted_iota(jnp.int32, (size, size), 1)
    same = (source // states) == (target % cols)
    upto = (source % states) <= (target // cols)
    sums = jnp.where(same & upto, 1.0, 0.0).astype(BF16)
    high, low = split(packed_s[...].T)
    total = jnp.dot(high, sums, preferred_element_type=F32) + jnp.dot(
        low, sums, preferred_element_type=F32
    )
    start = mid_ref[...].reshape(rows * chans, mid_ref.shape[2])[:, HALO : HALO + cols]
    here = states // tm
    start = jnp.concatenate([start] * here, 1)
    width = here * cols
    for k in range(tm):
        value = start + total[:, k * width : (k + 1) * width]
        for r in range(rows):
            chunk_s[k, :, r, :] = value[r * chans : (r + 1) * chans]
    for k in range(tm):
        outs[k][...] = chunk_s[my_tm ^ k]


def join_kernel(tm, *refs):
    blocks, out_ref, held = refs[:tm], refs[tm], refs[tm + 1]
    here = out_ref.shape[0]
    cols = out_ref.shape[3] // tm
    for k in range(tm):
        held[k] = blocks[k][...]
    my_tm = lax.axis_index("tm")
    for k in range(tm):
        block = held[my_tm ^ k]
        for t in range(here):
            out_ref[t, :, :, k * cols : (k + 1) * cols] = block[:, :, t * cols : (t + 1) * cols]


def kernel_call(body, out_shape, count, scratch=(), flops=0, read=0):
    vmem = pl.BlockSpec(memory_space=pltpu.VMEM)
    return pl.pallas_call(
        body,
        out_shape=out_shape,
        in_specs=[vmem] * count,
        out_specs=jax.tree.map(lambda _: vmem, out_shape),
        scratch_shapes=list(scratch),
        compiler_params=pltpu.CompilerParams(vmem_limit_bytes=VMEM_LIMIT),
        cost_estimate=pl.CostEstimate(flops=flops, bytes_accessed=read, transcendentals=0),
    )


def on_device(start_latent, time_embed, drift_x, drift_eps, w_in, b_in, w_mid, b_mid, w_out, b_out):
    tm, space = lax.axis_size("tm"), lax.axis_size("space")
    my_tm = lax.axis_index("tm")
    chans, rows, all_cols = start_latent.shape
    here, hid = time_embed.shape
    states, cols = here * tm, all_cols // tm
    depth = -(-(cols + 2 * HALO) // 128) * 128
    shape = jax.ShapeDtypeStruct

    padded = jnp.pad(start_latent, ((0, 0), (0, 0), (HALO, depth - cols - HALO)))
    mid = lax.dynamic_slice_in_dim(padded, my_tm * cols, depth, 2).transpose(1, 0, 2)
    up = lax.ppermute(mid[rows - HALO :], "space", [(i, i + 1) for i in range(space - 1)])
    down = lax.ppermute(mid[:HALO], "space", [(i + 1, i) for i in range(space - 1)])
    par = jnp.concatenate(
        [time_embed, drift_x[:, None], drift_eps[:, None], jnp.zeros((here, hid - 2), F32)], 1
    )
    par = lax.all_gather(par, "tm", tiled=True)

    wi = w_in.transpose(0, 3, 1, 2).reshape(3 * chans, 3 * hid)
    wo = w_out.transpose(0, 3, 1, 2).reshape(3, hid, 3 * chans)
    wo = jnp.concatenate([wo, wo, jnp.zeros((3, hid, hid - 6 * chans), F32)], 2)
    wi, wm, wo = kernel_call(
        weights_kernel,
        (
            shape((2 * hid, 3 * hid), BF16),
            shape((6, 6 * hid, 2 * hid), BF16),
            shape((6 * hid, hid), BF16),
        ),
        3,
        flops=10**7,
        read=3 * 10**6,
    )(wi, w_mid, wo)
    bias = jnp.stack([b_in, b_mid, jnp.tile(b_out, hid // chans)] + [b_in] * 5)

    groups = (cols + 8) // 4
    wide = 4 * groups
    width = here * cols
    chunks = kernel_call(
        functools.partial(main_kernel, tm),
        tuple(shape((chans, rows, width), F32) for _ in range(tm)),
        8,
        scratch=(
            pltpu.VMEM((rows + 2 * HALO, depth, hid), F32),
            pltpu.VMEM((6, rows + 10, groups * states, 2 * hid), BF16),
            pltpu.VMEM((rows + 8, wide * states, 2 * hid), BF16),
            pltpu.VMEM((rows + HALO, wide * states, hid), F32),
            pltpu.VMEM((cols * states, hid), F32),
            pltpu.VMEM((tm, chans, rows, width), F32),
            pltpu.VMEM((2, wide + 4, states, hid), F32),
            pltpu.VMEM((2, wide + 3, states, hid), F32),
            pltpu.VMEM((2, wide, states, hid), F32),
        ),
        flops=10**10,
        read=4 * 10**6,
    )(up, mid, down, par, bias, wi, wm, wo)

    blocks = [chunks[0]] + [
        lax.ppermute(chunks[k], "tm", [(i, i ^ k) for i in range(tm)]) for k in range(1, tm)
    ]
    return kernel_call(
        functools.partial(join_kernel, tm),
        shape((here, chans, rows, all_cols), F32),
        tm,
        scratch=(pltpu.VMEM((tm, chans, rows, width), F32),),
        read=10**6,
    )(*blocks)


def solution(mesh):
    in_specs = (
        P("group", "space", None),
        P("tm", None),
        P("tm"),
        P("tm"),
        P(),
        P(),
        P(),
        P(),
        P(),
        P(),
    )
    out_specs = P("tm", "group", "space", None)
    return jax.shard_map(
        on_device, mesh=mesh, in_specs=in_specs, out_specs=out_specs, check_vma=False
    )
```

```python
import functools
import jax
import jax.numpy as jnp
from jax import lax
from jax.experimental import pallas as pl
from jax.experimental.pallas import tpu as pltpu
from jax.sharding import PartitionSpec as P

REACH = 3
HALO = 2 * REACH
PACK = 8
NET = PACK - 2
OFF = -1e30
VMEM_LIMIT = 44 * 2**20
F32, BF16 = jnp.float32, jnp.bfloat16


def split(value):
    high = value.astype(BF16)
    return high, (value - high.astype(F32)).astype(BF16)


def silu_of_double(half):
    return half + half * jnp.tanh(half)


def lane_groups(shape, size):
    return lax.broadcasted_iota(jnp.int32, shape, len(shape) - 1) // size


def pack_kernel(start_ref, embed_ref, dx_ref, eps_ref, mid_ref, even_ref, odd_ref, par_ref):
    chans, rows, all_cols = start_ref.shape
    here, hid = embed_ref.shape
    first = lax.axis_index("tm") * (all_cols // lax.axis_size("tm")) - HALO
    shift = lax.rem(all_cols - first, all_cols)
    depth = mid_ref.shape[2]
    value = pltpu.roll(start_ref[...].reshape(chans * rows, all_cols), shift, 1)[:, :depth]
    place = lax.broadcasted_iota(jnp.int32, value.shape, 1) + first
    value = jnp.where((place >= 0) & (place < all_cols), value, 0.0)
    for c in range(chans):
        mid_ref[:, c, :] = value[c * rows : (c + 1) * rows]
    odd = lax.rem(lax.axis_index("space"), 2)
    even_ref[...] = mid_ref[pl.ds((1 - odd) * (rows - HALO), HALO)]
    odd_ref[...] = mid_ref[pl.ds(odd * (rows - HALO), HALO)]
    par_ref[:, :hid] = embed_ref[...]
    lane = lax.broadcasted_iota(jnp.int32, (1, hid), 1)
    for t in range(here):
        par_ref[t : t + 1, hid:] = jnp.where(
            lane == 0, dx_ref[t], jnp.where(lane == 1, eps_ref[t], 0.0)
        )


def weights_kernel(
    states, wi_ref, wm_ref, wo_ref, bi_ref, bm_ref, bo_ref,
    wi_out, wm_out, wo_out, wo_last, bias_out, sums_out,
):
    hid, chans = wi_ref.shape[2], wi_ref.shape[3]
    taps = [wi_ref[a, b] * 0.5 for a in range(3) for b in range(3)]
    first = jnp.concatenate(taps[:8], 1).T
    ninth = jnp.concatenate([taps[8]] * 8, 1).T
    taps = [first[t * chans : (t + 1) * chans] for t in range(8)] + [ninth[:chans]]
    terms = [split(jnp.concatenate(taps[3 * a : 3 * a + 3], 1)) for a in range(3)]
    high, low = [t[0] for t in terms], [t[1] for t in terms]
    none = jnp.zeros_like(high[0])
    upper = high + [none] + low + [none]
    lower = high + [none] * 5
    for r in range(NET):
        for g in range(PACK):
            at = (g + r) % PACK * chans
            wi_out[r, at : at + chans] = upper[g]
            wi_out[r, hid + at : hid + at + chans] = lower[g]
    for a in range(3):
        w0, w1, w2 = (wm_ref[a, b].T * 0.5 for b in range(3))
        even, odd = w0 * (1 / 24) + w2 * (1 / 6), w1 * (1 / 12)
        sides = (w0 + w2) * (-1 / 6)
        middle = w1 * (-1 / 6)
        forms = (w0 * 0.25, sides + middle, sides - middle, even + odd, even - odd, w2)
        for point, form in enumerate(forms):
            both = jnp.concatenate(split(form), 1)
            wm_out[point, 2 * a * hid : (2 * a + 1) * hid] = both
            wm_out[point, (2 * a + 1) * hid : (2 * a + 2) * hid] = both
    count = PACK + 2
    empty = jnp.zeros((chans, hid), F32)
    for k in range(count):
        for b in range(3):
            band = jnp.concatenate(
                [wo_ref[k - r, b] if 0 <= k - r < 3 else empty for r in range(PACK)], 0
            ).T
            high, low = split(band)
            if b < 2:
                lanes = slice(b * hid, (b + 1) * hid)
                wo_out[2 * k * hid : (2 * k + 1) * hid, lanes] = high
                wo_out[(2 * k + 1) * hid : (2 * k + 2) * hid, lanes] = high
                wo_out[(2 * count + k) * hid : (2 * count + k + 1) * hid, lanes] = low
            else:
                both = jnp.concatenate([high, low], 1)
                wo_last[2 * k * hid : (2 * k + 1) * hid] = both
                wo_last[(2 * k + 1) * hid : (2 * k + 2) * hid] = both
    bias_out[0:1] = bi_ref[...].reshape(1, hid) * 0.5
    bias_out[1:2] = bm_ref[...].reshape(1, hid) * 0.5
    bias_out[2:3] = jnp.concatenate([bo_ref[...].reshape(1, chans)] * PACK, 1)
    size = sums_out.shape[0]
    source = lax.broadcasted_iota(jnp.int32, (size, size), 0)
    target = lax.broadcasted_iota(jnp.int32, (size, size), 1)
    cols = size // states
    same = (source // states) == (target % cols)
    upto = (source % states) <= (target // cols)
    sums_out[...] = jnp.where(same & upto, 1.0, 0.0).astype(BF16)


def main_kernel(tm, *refs):
    mid_ref, even_ref, odd_ref = refs[:3]
    pars = refs[3 : 3 + tm]
    bias_ref, wi_ref, wm_ref, wo_ref, wo_last, sums_ref = refs[3 + tm : 9 + tm]
    outs = refs[9 + tm : 9 + 2 * tm]
    (
        rows_s, par_s, held_s, start_s, common_s, points_s, hid2_s, inputs_s, chunk_s,
        in_bias, mid_bias, eps_s,
    ) = refs[9 + 2 * tm :]
    rows, chans, depth = mid_ref.shape
    states, hid = par_s.shape[0], par_s.shape[1] // 2
    groups = points_s.shape[2] // states
    wide = 4 * groups
    cols = wide - 8
    my_tm, my_space = lax.axis_index("tm"), lax.axis_index("space")
    all_rows, all_cols = rows * lax.axis_size("space"), cols * tm
    row0, col0 = my_space * rows, my_tm * cols

    here = states // tm
    for k in range(tm):
        held_s[k] = pars[k][...]
    for k in range(tm):
        par_s[k * here : (k + 1) * here] = held_s[my_tm ^ k]

    embed = par_s[:, :hid]
    drift_x = jnp.broadcast_to(par_s[:, hid : hid + 1], (states, hid))
    drift_eps = jnp.broadcast_to(par_s[:, hid + 1 : hid + 2], (states, hid))

    def inside(first, width, limit):
        place = lax.broadcasted_iota(jnp.int32, (width, states, hid), 0)
        return (place + first >= 0) & (place + first < all_cols) & (place < limit)

    bias = bias_ref[0:1] + 0.5 * embed
    in_bias[0] = jnp.full(in_bias.shape[1:], OFF, F32)
    in_bias[1] = jnp.where(inside(col0 - 5, wide + 4, wide + 2), bias[None], OFF)
    mid_bias[0] = jnp.full(mid_bias.shape[1:], OFF, F32)
    mid_bias[1] = jnp.where(
        inside(col0 - 4, wide + 3, wide + 3),
        jnp.broadcast_to(bias_ref[1:2], (states, hid))[None],
        OFF,
    )
    reach_cols = cols + HALO
    eps_s[...] = jnp.where(inside(col0 - 3, reach_cols, reach_cols), drift_eps[None], 0.0)
    out_bias = bias_ref[2:3]

    def in_field(row):
        return jnp.where((row >= 0) & (row < all_rows), 1, 0)

    odd = lax.rem(my_space, 2) == 1
    rows_s[:HALO] = jnp.where(odd, even_ref[...], odd_ref[...])
    rows_s[HALO : HALO + rows] = mid_ref[...]
    rows_s[HALO + rows :] = jnp.where(odd, odd_ref[...], even_ref[...])

    def packed_start(first):
        return rows_s[first : first + PACK].reshape(PACK * chans, depth).T

    def first_conv(r, values):
        group = lane_groups(values[0].shape, chans)
        own = (group >= r) & (group <= r + 2)
        left = []
        for value in values:
            turned = pltpu.roll(value, hid // 2, 1)
            low = split(value)[1]
            left.append(jnp.concatenate([jnp.where(own, value, turned).astype(BF16), low], 1))
        return jnp.dot(jnp.concatenate(left, 0), wi_ref[r], preferred_element_type=F32)

    def to_points(row, field):
        fours = field.reshape(groups + 1, 4, states, hid)
        d0, d1, d2, d3 = (fours[:groups, k] for k in range(4))
        d4, d5 = fours[1:, 0], fours[1:, 1]
        e1, e2 = d4 - 4 * d2, d3 - 4 * d1
        e3, e4 = d4 - d2, 2 * (d3 - d1)
        forms = (4 * (d0 - d2) + e3, e1 + e2, e1 - e2, e3 + e4, e3 - e4, (d5 - d3) - 2 * e4)
        for point, form in enumerate(forms):
            high, low = split(form.reshape(groups * states, hid))
            points_s[point, row, :, :hid] = high
            points_s[point, row, :, hid:] = low

    def second_hidden(count, step, row_first, col_first):
        def body(c, _):
            first = c * step
            sums = []
            for point in range(6):
                left = jnp.concatenate(
                    [
                        points_s[point, pl.ds(first + a, step)].reshape(step * groups * states, 2 * hid)
                        for a in range(3)
                    ],
                    1,
                )
                both = jnp.dot(left, wm_ref[point], preferred_element_type=F32)
                sums.append((both[:, :hid] + both[:, hid:]).reshape(step, groups, states, hid))
            m0, m1, m2, m3, m4, m5 = sums
            s1, t1, s3, t3 = m1 + m2, m1 - m2, m3 + m4, m3 - m4
            field = jnp.stack(
                [m0 + s1 + s3, t1 + 2 * t3, s1 + 4 * s3, t1 + 8 * t3 + m5], 2
            ).reshape(step, wide, states, hid)
            for r in range(step):
                ok = in_field(row0 + row_first + first + r)
                value = silu_of_double(field[r] + mid_bias[ok, col_first : col_first + wide])
                high, low = split(value.reshape(wide * states, hid))
                hid2_s[first + r, :, :hid] = high
                hid2_s[first + r, :, hid:] = low
            return 0

        lax.fori_loop(0, count // step, body, 0)

    def noise(packs, width):
        count = PACK + 2
        both = [
            jnp.concatenate([hid2_s[NET * p + k] for p in range(packs)], 0) for k in range(count)
        ]
        left = jnp.concatenate(both + [v[:, :hid] for v in both], 1)
        two = jnp.dot(left, wo_ref[...], preferred_element_type=F32)
        last = jnp.dot(left[:, : 2 * count * hid], wo_last[...], preferred_element_type=F32)
        shape = (packs, wide, states, hid)
        t0, t1 = two[:, :hid].reshape(shape), two[:, hid:].reshape(shape)
        t2 = (last[:, :hid] + last[:, hid:]).reshape(shape)
        return t0[:, :width] + t1[:, 1 : width + 1] + t2[:, 2 : width + 2] + out_bias

    state = lax.broadcasted_iota(jnp.int32, (1, states, hid), 1)

    def earlier(value):
        value = jnp.where(state >= 1, pltpu.roll(value, 1, 1), 0.0)
        reach = 1
        while reach < states:
            value = value + jnp.where(state >= reach, pltpu.roll(value, reach, 1), 0.0)
            reach *= 2
        return value

    packs = start_s.shape[0]
    for p in range(packs):
        start_s[p] = packed_start(NET * p)

    def first_rows(r, _):
        taps = first_conv(r, [start_s[p] for p in range(packs)])
        for p in range(packs):
            t0, t1, t2 = (
                taps[p * depth : (p + 1) * depth, k * hid : (k + 1) * hid] for k in range(3)
            )
            common_s[NET * p + r] = t0 + pltpu.roll(t1, depth - 1, 0) + pltpu.roll(t2, depth - 2, 0)
        return 0

    lax.fori_loop(0, NET, first_rows, 0)

    def first_points(i, _):
        ok = in_field(row0 - 5 + i)
        to_points(i, silu_of_double(common_s[i, : wide + 4][:, None, :] + in_bias[ok]))
        return 0

    lax.fori_loop(0, rows + 10, first_points, 0)
    second_hidden(rows + 8, 4, -4, 0)

    packs = inputs_s.shape[0]
    value = noise(packs, reach_cols)
    group = lane_groups((1, hid), chans)
    for p in range(packs):
        start = packed_start(REACH + NET * p)[REACH : REACH + reach_cols]
        start = jnp.broadcast_to(start[:, None, :], (reach_cols, states, hid))
        row = group + (row0 - REACH + NET * p)
        keep = jnp.where((row >= 0) & (row < all_rows), 1.0, 0.0)
        drift = drift_x[None] * start + eps_s[...] * (value[p] * keep)
        total = (start + earlier(drift)).reshape(reach_cols * states, hid)
        inputs_s[p, : reach_cols * states] = total
        inputs_s[p, reach_cols * states :] = jnp.zeros(((wide - reach_cols) * states, hid), F32)

    def second_rows(r, _):
        taps = first_conv(r, [inputs_s[p] for p in range(packs)])
        width = cols + 4
        for p in range(packs):
            first = p * wide * states
            t0, t1, t2 = (
                taps[first + k * states : first + (k + width) * states, k * hid : (k + 1) * hid]
                for k in range(3)
            )
            i = NET * p + r
            ok = in_field(row0 - 2 + i)
            value = (t0 + t1 + t2).reshape(width, states, hid) + in_bias[ok, 3 : 3 + width]
            value = silu_of_double(value)
            to_points(i, jnp.concatenate([value, jnp.zeros((8, states, hid), F32)], 0))
        return 0

    lax.fori_loop(0, NET, second_rows, 0)
    second_hidden(rows + 2, 5, -1, 3)

    value = noise(1, cols)[0]
    size = cols * states
    upper = inputs_s[0, REACH * states : REACH * states + size]
    lower = inputs_s[1, REACH * states : REACH * states + size]
    inputs = jnp.where(
        lane_groups((size, hid), chans) < PACK - REACH,
        pltpu.roll(upper, hid - REACH * chans, 1),
        pltpu.roll(lower, (NET - REACH) * chans, 1),
    ).reshape(cols, states, hid)
    drift = drift_x[None] * inputs + drift_eps[None] * value
    high, low = split(drift.reshape(size, hid).T)
    total = jnp.dot(high, sums_ref[...], preferred_element_type=F32) + jnp.dot(
        low, sums_ref[...], preferred_element_type=F32
    )
    start = mid_ref[...].reshape(rows * chans, depth)[:, HALO : HALO + cols]
    start = jnp.concatenate([start] * here, 1)
    width = here * cols
    for k in range(tm):
        value = start + total[:, k * width : (k + 1) * width]
        for r in range(rows):
            chunk_s[k, :, r, :] = value[r * chans : (r + 1) * chans]
    for k in range(tm):
        outs[k][...] = chunk_s[my_tm ^ k]


def join_kernel(tm, *refs):
    blocks, out_ref, held = refs[:tm], refs[tm], refs[tm + 1]
    here = out_ref.shape[0]
    cols = out_ref.shape[3] // tm
    for k in range(tm):
        held[k] = blocks[k][...]
    my_tm = lax.axis_index("tm")
    for k in range(tm):
        block = held[my_tm ^ k]
        for t in range(here):
            out_ref[t, :, :, k * cols : (k + 1) * cols] = block[:, :, t * cols : (t + 1) * cols]


def kernel_call(body, out_shape, in_specs, scratch=(), flops=0, read=0):
    vmem = pl.BlockSpec(memory_space=pltpu.VMEM)
    if isinstance(in_specs, int):
        in_specs = [vmem] * in_specs
    return pl.pallas_call(
        body,
        out_shape=out_shape,
        in_specs=in_specs,
        out_specs=jax.tree.map(lambda _: vmem, out_shape),
        scratch_shapes=list(scratch),
        compiler_params=pltpu.CompilerParams(vmem_limit_bytes=VMEM_LIMIT),
        cost_estimate=pl.CostEstimate(flops=flops, bytes_accessed=read, transcendentals=0),
    )


def on_device(start_latent, time_embed, drift_x, drift_eps, w_in, b_in, w_mid, b_mid, w_out, b_out):
    tm, space = lax.axis_size("tm"), lax.axis_size("space")
    chans, rows, all_cols = start_latent.shape
    here, hid = time_embed.shape
    states, cols = here * tm, all_cols // tm
    depth = -(-(cols + 2 * HALO) // 128) * 128
    assert rows == PACK and hid == PACK * chans
    shape = jax.ShapeDtypeStruct
    vmem, smem = (pl.BlockSpec(memory_space=m) for m in (pltpu.VMEM, pltpu.SMEM))

    edge = shape((HALO, chans, depth), F32)
    mid, even, odd, par = kernel_call(
        pack_kernel,
        (shape((rows, chans, depth), F32), edge, edge, shape((here, 2 * hid), F32)),
        [vmem, vmem, smem, smem],
        read=10**6,
    )(start_latent, time_embed, drift_x, drift_eps)
    even = lax.ppermute(even, "space", [(i, i ^ 1) for i in range(space) if i ^ 1 < space])
    pairs = [(i, i + 1) for i in range(1, space - 1, 2)]
    odd = lax.ppermute(odd, "space", pairs + [(b, a) for a, b in pairs])
    pars = [par] + [
        lax.ppermute(par, "tm", [(i, i ^ k) for i in range(tm)]) for k in range(1, tm)
    ]

    taps = (PACK + 2) * hid
    weights = kernel_call(
        functools.partial(weights_kernel, states),
        (
            shape((NET, 2 * hid, 3 * hid), BF16),
            shape((6, 6 * hid, 2 * hid), BF16),
            shape((3 * taps, 2 * hid), BF16),
            shape((2 * taps, 2 * hid), BF16),
            shape((8, hid), F32),
            shape((cols * states, cols * states), BF16),
        ),
        6,
        flops=10**7,
        read=8 * 10**6,
    )(w_in, w_mid, w_out, b_in, b_mid, b_out)
    wi, wm, wo, wo_last, bias, sums = weights

    groups = (cols + 8) // 4
    wide = 4 * groups
    width = here * cols
    chunks = kernel_call(
        functools.partial(main_kernel, tm),
        tuple(shape((chans, rows, width), F32) for _ in range(tm)),
        9 + tm,
        scratch=(
            pltpu.VMEM((rows + 2 * HALO, chans, depth), F32),
            pltpu.VMEM((states, 2 * hid), F32),
            pltpu.VMEM((tm, here, 2 * hid), F32),
            pltpu.VMEM(((rows + 2 * HALO - 2) // NET, depth, hid), F32),
            pltpu.VMEM((rows + 10, depth, hid), F32),
            pltpu.VMEM((6, rows + 10, groups * states, 2 * hid), BF16),
            pltpu.VMEM((rows + 8, wide * states, 2 * hid), BF16),
            pltpu.VMEM(((rows + HALO - 2) // NET, wide * states, hid), F32),
            pltpu.VMEM((tm, chans, rows, width), F32),
            pltpu.VMEM((2, wide + 4, states, hid), F32),
            pltpu.VMEM((2, wide + 3, states, hid), F32),
            pltpu.VMEM((cols + HALO, states, hid), F32),
        ),
        flops=10**10,
        read=8 * 10**6,
    )(mid, even, odd, *pars, bias, wi, wm, wo, wo_last, sums)

    blocks = [chunks[0]] + [
        lax.ppermute(chunks[k], "tm", [(i, i ^ k) for i in range(tm)]) for k in range(1, tm)
    ]
    return kernel_call(
        functools.partial(join_kernel, tm),
        shape((here, chans, rows, all_cols), F32),
        tm,
        scratch=(pltpu.VMEM((tm, chans, rows, width), F32),),
        read=10**6,
    )(*blocks)


def solution(mesh):
    in_specs = (
        P("group", "space", None),
        P("tm", None),
        P("tm"),
        P("tm"),
        P(),
        P(),
        P(),
        P(),
        P(),
        P(),
    )
    out_specs = P("tm", "group", "space", None)
    return jax.shard_map(
        on_device, mesh=mesh, in_specs=in_specs, out_specs=out_specs, check_vma=False
    )
```

```python
import functools
import jax
import jax.numpy as jnp
from jax import lax
from jax.experimental import pallas as pl
from jax.experimental.pallas import tpu as pltpu
from jax.sharding import PartitionSpec as P

REACH = 3
HALO = 2 * REACH
PACK = 8
NET = PACK - 2
OFF = -1e30
VMEM_LIMIT = 44 * 2**20
F32, BF16 = jnp.float32, jnp.bfloat16


def split(value):
    high = value.astype(BF16)
    return high, (value - high.astype(F32)).astype(BF16)


def silu_of_double(half):
    return half + half * jnp.tanh(half)


def lane_groups(shape, size):
    return lax.broadcasted_iota(jnp.int32, shape, len(shape) - 1) // size


def fetch(sources, targets, sems):
    copies = [
        pltpu.make_async_copy(source, target, sems.at[k])
        for k, (source, target) in enumerate(zip(sources, targets))
    ]
    for copy in copies:
        copy.start()
    return copies


def arrive(copies):
    for copy in copies:
        copy.wait()


def pack_kernel(*refs):
    sources, (mid_ref, even_ref, odd_ref, par_ref) = refs[:4], refs[4:8]
    start_ref, embed_ref, dx_ref, eps_ref = refs[8:12]
    arrive(fetch(sources, refs[8:12], refs[12]))
    chans, rows, all_cols = start_ref.shape
    here, hid = embed_ref.shape
    first = lax.axis_index("tm") * (all_cols // lax.axis_size("tm")) - HALO
    shift = lax.rem(all_cols - first, all_cols)
    depth = mid_ref.shape[2]
    value = pltpu.roll(start_ref[...].reshape(chans * rows, all_cols), shift, 1)[:, :depth]
    place = lax.broadcasted_iota(jnp.int32, value.shape, 1) + first
    value = jnp.where((place >= 0) & (place < all_cols), value, 0.0)
    for c in range(chans):
        mid_ref[:, c, :] = value[c * rows : (c + 1) * rows]
    odd = lax.rem(lax.axis_index("space"), 2)
    even_ref[...] = mid_ref[pl.ds((1 - odd) * (rows - HALO), HALO)]
    odd_ref[...] = mid_ref[pl.ds(odd * (rows - HALO), HALO)]
    par_ref[:, :hid] = embed_ref[...]
    lane = lax.broadcasted_iota(jnp.int32, (1, hid), 1)
    for t in range(here):
        par_ref[t : t + 1, hid:] = jnp.where(
            lane == 0, dx_ref[t], jnp.where(lane == 1, eps_ref[t], 0.0)
        )


def weights_kernel(states, *refs):
    wi_out, wm_out, wo_out, wo_last, bias_out, sums_out = refs[6:12]
    wi_ref, wm_ref, wo_ref, bi_ref, bm_ref, bo_ref = refs[12:18]
    arrive(fetch(refs[:6], refs[12:18], refs[18]))
    chans, hid = wi_ref.shape[2], wi_ref.shape[3]
    terms = [split(jnp.concatenate([wi_ref[a, b] * 0.5 for b in range(3)], 1)) for a in range(3)]
    high, low = [t[0] for t in terms], [t[1] for t in terms]
    none = jnp.zeros_like(high[0])
    upper = high + [none] + low + [none]
    lower = high + [none] * 5
    for r in range(NET):
        for g in range(PACK):
            at = (g + r) % PACK * chans
            wi_out[r, at : at + chans] = upper[g]
            wi_out[r, hid + at : hid + at + chans] = lower[g]
    for a in range(3):
        w0, w1, w2 = (wm_ref[a, b].T * 0.5 for b in range(3))
        even, odd = w0 * (1 / 24) + w2 * (1 / 6), w1 * (1 / 12)
        sides = (w0 + w2) * (-1 / 6)
        middle = w1 * (-1 / 6)
        forms = (w0 * 0.25, sides + middle, sides - middle, even + odd, even - odd, w2)
        for point, form in enumerate(forms):
            both = jnp.concatenate(split(form), 1)
            wm_out[point, 2 * a * hid : (2 * a + 1) * hid] = both
            wm_out[point, (2 * a + 1) * hid : (2 * a + 2) * hid] = both
    count = PACK + 2
    empty = jnp.zeros((chans, hid), F32)
    for k in range(count):
        for b in range(3):
            band = jnp.concatenate(
                [wo_ref[k - r, b] if 0 <= k - r < 3 else empty for r in range(PACK)], 0
            ).T
            high, low = split(band)
            if b < 2:
                lanes = slice(b * hid, (b + 1) * hid)
                wo_out[2 * k * hid : (2 * k + 1) * hid, lanes] = high
                wo_out[(2 * k + 1) * hid : (2 * k + 2) * hid, lanes] = high
                wo_out[(2 * count + k) * hid : (2 * count + k + 1) * hid, lanes] = low
            else:
                both = jnp.concatenate([high, low], 1)
                wo_last[2 * k * hid : (2 * k + 1) * hid] = both
                wo_last[(2 * k + 1) * hid : (2 * k + 2) * hid] = both
    bias_out[0:1] = bi_ref[...].reshape(1, hid) * 0.5
    bias_out[1:2] = bm_ref[...].reshape(1, hid) * 0.5
    bias_out[2:3] = jnp.concatenate([bo_ref[...].reshape(1, chans)] * PACK, 1)
    size = sums_out.shape[0]
    source = lax.broadcasted_iota(jnp.int32, (size, size), 0)
    target = lax.broadcasted_iota(jnp.int32, (size, size), 1)
    cols = size // states
    same = (source // states) == (target % cols)
    upto = (source % states) <= (target // cols)
    sums_out[...] = jnp.where(same & upto, 1.0, 0.0).astype(BF16)


def main_kernel(tm, *refs):
    mid_ref, even_ref, odd_ref = refs[:3]
    pars = refs[3 : 3 + tm]
    bias_ref, wi_ref, wm_ref, wo_ref, wo_last, sums_ref = refs[3 + tm : 9 + tm]
    outs = refs[9 + tm : 9 + 2 * tm]
    (
        rows_s, par_s, held_s, start_s, common_s, points_s, hid2_s, inputs_s, chunk_s,
        in_bias, mid_bias, eps_s,
    ) = refs[9 + 2 * tm :]
    rows, chans, depth = mid_ref.shape
    states, hid = par_s.shape[0], par_s.shape[1] // 2
    groups = points_s.shape[2] // states
    wide = 4 * groups
    cols = wide - 8
    my_tm, my_space = lax.axis_index("tm"), lax.axis_index("space")
    all_rows, all_cols = rows * lax.axis_size("space"), cols * tm
    row0, col0 = my_space * rows, my_tm * cols

    here = states // tm
    for k in range(tm):
        held_s[k] = pars[k][...]
    for k in range(tm):
        par_s[k * here : (k + 1) * here] = held_s[my_tm ^ k]

    embed = par_s[:, :hid]
    drift_x = jnp.broadcast_to(par_s[:, hid : hid + 1], (states, hid))
    drift_eps = jnp.broadcast_to(par_s[:, hid + 1 : hid + 2], (states, hid))

    def inside(first, width, limit):
        place = lax.broadcasted_iota(jnp.int32, (width, states, hid), 0)
        return (place + first >= 0) & (place + first < all_cols) & (place < limit)

    bias = bias_ref[0:1] + 0.5 * embed
    in_bias[0] = jnp.full(in_bias.shape[1:], OFF, F32)
    in_bias[1] = jnp.where(inside(col0 - 5, wide + 4, wide + 2), bias[None], OFF)
    mid_bias[0] = jnp.full(mid_bias.shape[1:], OFF, F32)
    mid_bias[1] = jnp.where(
        inside(col0 - 4, wide + 3, wide + 3),
        jnp.broadcast_to(bias_ref[1:2], (states, hid))[None],
        OFF,
    )
    reach_cols = cols + HALO
    eps_s[...] = jnp.where(inside(col0 - 3, reach_cols, reach_cols), drift_eps[None], 0.0)
    out_bias = bias_ref[2:3]

    def in_field(row):
        return jnp.where((row >= 0) & (row < all_rows), 1, 0)

    odd = lax.rem(my_space, 2) == 1
    rows_s[:HALO] = jnp.where(odd, even_ref[...], odd_ref[...])
    rows_s[HALO : HALO + rows] = mid_ref[...]
    rows_s[HALO + rows :] = jnp.where(odd, odd_ref[...], even_ref[...])

    def packed_start(first):
        return rows_s[first : first + PACK].reshape(PACK * chans, depth).T

    def first_conv(r, values):
        group = lane_groups(values[0].shape, chans)
        own = (group >= r) & (group <= r + 2)
        left = []
        for value in values:
            turned = pltpu.roll(value, hid // 2, 1)
            low = split(value)[1]
            left.append(jnp.concatenate([jnp.where(own, value, turned).astype(BF16), low], 1))
        return jnp.dot(jnp.concatenate(left, 0), wi_ref[r], preferred_element_type=F32)

    def to_points(row, field):
        fours = field.reshape(groups + 1, 4, states, hid)
        d0, d1, d2, d3 = (fours[:groups, k] for k in range(4))
        d4, d5 = fours[1:, 0], fours[1:, 1]
        e1, e2 = d4 - 4 * d2, d3 - 4 * d1
        e3, e4 = d4 - d2, 2 * (d3 - d1)
        forms = (4 * (d0 - d2) + e3, e1 + e2, e1 - e2, e3 + e4, e3 - e4, (d5 - d3) - 2 * e4)
        for point, form in enumerate(forms):
            high, low = split(form.reshape(groups * states, hid))
            points_s[point, row, :, :hid] = high
            points_s[point, row, :, hid:] = low

    def second_hidden(count, step, row_first, col_first):
        def body(c, _):
            first = c * step
            sums = []
            for point in range(6):
                left = jnp.concatenate(
                    [
                        points_s[point, pl.ds(first + a, step)].reshape(step * groups * states, 2 * hid)
                        for a in range(3)
                    ],
                    1,
                )
                both = jnp.dot(left, wm_ref[point], preferred_element_type=F32)
                sums.append((both[:, :hid] + both[:, hid:]).reshape(step, groups, states, hid))
            m0, m1, m2, m3, m4, m5 = sums
            s1, t1, s3, t3 = m1 + m2, m1 - m2, m3 + m4, m3 - m4
            field = jnp.stack(
                [m0 + s1 + s3, t1 + 2 * t3, s1 + 4 * s3, t1 + 8 * t3 + m5], 2
            ).reshape(step, wide, states, hid)
            for r in range(step):
                ok = in_field(row0 + row_first + first + r)
                value = silu_of_double(field[r] + mid_bias[ok, col_first : col_first + wide])
                high, low = split(value.reshape(wide * states, hid))
                hid2_s[first + r, :, :hid] = high
                hid2_s[first + r, :, hid:] = low
            return 0

        lax.fori_loop(0, count // step, body, 0)

    def noise(packs, width):
        count = PACK + 2
        both = [
            jnp.concatenate([hid2_s[NET * p + k] for p in range(packs)], 0) for k in range(count)
        ]
        left = jnp.concatenate(both + [v[:, :hid] for v in both], 1)
        two = jnp.dot(left, wo_ref[...], preferred_element_type=F32)
        last = jnp.dot(left[:, : 2 * count * hid], wo_last[...], preferred_element_type=F32)
        shape = (packs, wide, states, hid)
        t0, t1 = two[:, :hid].reshape(shape), two[:, hid:].reshape(shape)
        t2 = (last[:, :hid] + last[:, hid:]).reshape(shape)
        return t0[:, :width] + t1[:, 1 : width + 1] + t2[:, 2 : width + 2] + out_bias

    state = lax.broadcasted_iota(jnp.int32, (1, states, hid), 1)

    def earlier(value):
        value = jnp.where(state >= 1, pltpu.roll(value, 1, 1), 0.0)
        reach = 1
        while reach < states:
            value = value + jnp.where(state >= reach, pltpu.roll(value, reach, 1), 0.0)
            reach *= 2
        return value

    packs = start_s.shape[0]
    for p in range(packs):
        start_s[p] = packed_start(NET * p)

    def first_rows(r, _):
        taps = first_conv(r, [start_s[p] for p in range(packs)])
        for p in range(packs):
            t0, t1, t2 = (
                taps[p * depth : (p + 1) * depth, k * hid : (k + 1) * hid] for k in range(3)
            )
            common_s[NET * p + r] = t0 + pltpu.roll(t1, depth - 1, 0) + pltpu.roll(t2, depth - 2, 0)
        return 0

    lax.fori_loop(0, NET, first_rows, 0)

    def first_points(i, _):
        ok = in_field(row0 - 5 + i)
        to_points(i, silu_of_double(common_s[i, : wide + 4][:, None, :] + in_bias[ok]))
        return 0

    lax.fori_loop(0, rows + 10, first_points, 0)
    second_hidden(rows + 8, 4, -4, 0)

    packs = inputs_s.shape[0]
    value = noise(packs, reach_cols)
    group = lane_groups((1, hid), chans)
    for p in range(packs):
        start = packed_start(REACH + NET * p)[REACH : REACH + reach_cols]
        start = jnp.broadcast_to(start[:, None, :], (reach_cols, states, hid))
        row = group + (row0 - REACH + NET * p)
        keep = jnp.where((row >= 0) & (row < all_rows), 1.0, 0.0)
        drift = drift_x[None] * start + eps_s[...] * (value[p] * keep)
        total = (start + earlier(drift)).reshape(reach_cols * states, hid)
        inputs_s[p, : reach_cols * states] = total
        inputs_s[p, reach_cols * states :] = jnp.zeros(((wide - reach_cols) * states, hid), F32)

    def second_rows(r, _):
        taps = first_conv(r, [inputs_s[p] for p in range(packs)])
        width = cols + 4
        for p in range(packs):
            first = p * wide * states
            t0, t1, t2 = (
                taps[first + k * states : first + (k + width) * states, k * hid : (k + 1) * hid]
                for k in range(3)
            )
            i = NET * p + r
            ok = in_field(row0 - 2 + i)
            value = (t0 + t1 + t2).reshape(width, states, hid) + in_bias[ok, 3 : 3 + width]
            value = silu_of_double(value)
            to_points(i, jnp.concatenate([value, jnp.zeros((8, states, hid), F32)], 0))
        return 0

    lax.fori_loop(0, NET, second_rows, 0)
    second_hidden(rows + 2, 5, -1, 3)

    value = noise(1, cols)[0]
    size = cols * states
    upper = inputs_s[0, REACH * states : REACH * states + size]
    lower = inputs_s[1, REACH * states : REACH * states + size]
    inputs = jnp.where(
        lane_groups((size, hid), chans) < PACK - REACH,
        pltpu.roll(upper, hid - REACH * chans, 1),
        pltpu.roll(lower, (NET - REACH) * chans, 1),
    ).reshape(cols, states, hid)
    drift = drift_x[None] * inputs + drift_eps[None] * value
    high, low = split(drift.reshape(size, hid).T)
    total = jnp.dot(high, sums_ref[...], preferred_element_type=F32) + jnp.dot(
        low, sums_ref[...], preferred_element_type=F32
    )
    start = mid_ref[...].reshape(rows * chans, depth)[:, HALO : HALO + cols]
    start = jnp.concatenate([start] * here, 1)
    width = here * cols
    for k in range(tm):
        value = start + total[:, k * width : (k + 1) * width]
        for r in range(rows):
            chunk_s[k, :, r, :] = value[r * chans : (r + 1) * chans]
    for k in range(tm):
        outs[k][...] = chunk_s[my_tm ^ k]


def join_kernel(tm, *refs):
    blocks, out_ref, held = refs[:tm], refs[tm], refs[tm + 1]
    here = out_ref.shape[0]
    cols = out_ref.shape[3] // tm
    for k in range(tm):
        held[k] = blocks[k][...]
    my_tm = lax.axis_index("tm")
    for k in range(tm):
        block = held[my_tm ^ k]
        for t in range(here):
            out_ref[t, :, :, k * cols : (k + 1) * cols] = block[:, :, t * cols : (t + 1) * cols]


def kernel_call(body, out_shape, in_specs, scratch=(), flops=0, read=0):
    vmem = pl.BlockSpec(memory_space=pltpu.VMEM)
    if isinstance(in_specs, int):
        in_specs = [vmem] * in_specs
    return pl.pallas_call(
        body,
        out_shape=out_shape,
        in_specs=in_specs,
        out_specs=jax.tree.map(lambda _: vmem, out_shape),
        scratch_shapes=list(scratch),
        compiler_params=pltpu.CompilerParams(vmem_limit_bytes=VMEM_LIMIT),
        cost_estimate=pl.CostEstimate(flops=flops, bytes_accessed=read, transcendentals=0),
    )


def in_hbm(value):
    return pltpu.with_memory_space_constraint(value, pltpu.HBM)


def on_device(start_latent, time_embed, drift_x, drift_eps, w_in, b_in, w_mid, b_mid, w_out, b_out):
    tm, space = lax.axis_size("tm"), lax.axis_size("space")
    chans, rows, all_cols = start_latent.shape
    here, hid = time_embed.shape
    states, cols = here * tm, all_cols // tm
    depth = -(-(cols + 2 * HALO) // 128) * 128
    assert rows == PACK and hid == PACK * chans
    shape, local = jax.ShapeDtypeStruct, pltpu.VMEM
    hbm = pl.BlockSpec(memory_space=pltpu.HBM)

    edge = local((HALO, chans, depth), F32)
    mid, even, odd, par = kernel_call(
        pack_kernel,
        (local((rows, chans, depth), F32), edge, edge, local((here, 2 * hid), F32)),
        [hbm] * 4,
        scratch=(
            pltpu.VMEM((chans, rows, all_cols), F32),
            pltpu.VMEM((here, hid), F32),
            pltpu.SMEM((here,), F32),
            pltpu.SMEM((here,), F32),
            pltpu.SemaphoreType.DMA((4,)),
        ),
        read=10**6,
    )(*map(in_hbm, (start_latent, time_embed, drift_x, drift_eps)))
    even = lax.ppermute(even, "space", [(i, i ^ 1) for i in range(space) if i ^ 1 < space])
    pairs = [(i, i + 1) for i in range(1, space - 1, 2)]
    odd = lax.ppermute(odd, "space", pairs + [(b, a) for a, b in pairs])
    pars = [par] + [
        lax.ppermute(par, "tm", [(i, i ^ k) for i in range(tm)]) for k in range(1, tm)
    ]

    taps = (PACK + 2) * hid
    weights = kernel_call(
        functools.partial(weights_kernel, states),
        (
            local((NET, 2 * hid, 3 * hid), BF16),
            local((6, 6 * hid, 2 * hid), BF16),
            local((3 * taps, 2 * hid), BF16),
            local((2 * taps, 2 * hid), BF16),
            local((8, hid), F32),
            local((cols * states, cols * states), BF16),
        ),
        [hbm] * 6,
        scratch=(
            pltpu.VMEM((3, 3, chans, hid), F32),
            pltpu.VMEM((3, 3, hid, hid), F32),
            pltpu.VMEM((3, 3, chans, hid), F32),
            pltpu.VMEM((hid,), F32),
            pltpu.VMEM((hid,), F32),
            pltpu.VMEM((chans,), F32),
            pltpu.SemaphoreType.DMA((6,)),
        ),
        flops=10**7,
        read=8 * 10**6,
    )(*map(in_hbm, (w_in.transpose(0, 1, 3, 2), w_mid, w_out, b_in, b_mid, b_out)))
    wi, wm, wo, wo_last, bias, sums = weights

    groups = (cols + 8) // 4
    wide = 4 * groups
    width = here * cols
    chunks = kernel_call(
        functools.partial(main_kernel, tm),
        tuple(local((chans, rows, width), F32) for _ in range(tm)),
        9 + tm,
        scratch=(
            pltpu.VMEM((rows + 2 * HALO, chans, depth), F32),
            pltpu.VMEM((states, 2 * hid), F32),
            pltpu.VMEM((tm, here, 2 * hid), F32),
            pltpu.VMEM(((rows + 2 * HALO - 2) // NET, depth, hid), F32),
            pltpu.VMEM((rows + 10, depth, hid), F32),
            pltpu.VMEM((6, rows + 10, groups * states, 2 * hid), BF16),
            pltpu.VMEM((rows + 8, wide * states, 2 * hid), BF16),
            pltpu.VMEM(((rows + HALO - 2) // NET, wide * states, hid), F32),
            pltpu.VMEM((tm, chans, rows, width), F32),
            pltpu.VMEM((2, wide + 4, states, hid), F32),
            pltpu.VMEM((2, wide + 3, states, hid), F32),
            pltpu.VMEM((cols + HALO, states, hid), F32),
        ),
        flops=10**10,
        read=8 * 10**6,
    )(mid, even, odd, *pars, bias, wi, wm, wo, wo_last, sums)

    blocks = [chunks[0]] + [
        lax.ppermute(chunks[k], "tm", [(i, i ^ k) for i in range(tm)]) for k in range(1, tm)
    ]
    return kernel_call(
        functools.partial(join_kernel, tm),
        shape((here, chans, rows, all_cols), F32),
        tm,
        scratch=(pltpu.VMEM((tm, chans, rows, width), F32),),
        read=10**6,
    )(*blocks)


def solution(mesh):
    in_specs = (
        P("group", "space", None),
        P("tm", None),
        P("tm"),
        P("tm"),
        P(),
        P(),
        P(),
        P(),
        P(),
        P(),
    )
    out_specs = P("tm", "group", "space", None)
    return jax.shard_map(
        on_device, mesh=mesh, in_specs=in_specs, out_specs=out_specs, check_vma=False
    )
```

```python
import functools
import jax
import jax.numpy as jnp
from jax import lax
from jax.experimental import pallas as pl
from jax.experimental.pallas import tpu as pltpu
from jax.sharding import PartitionSpec as P

REACH = 3
HALO = 2 * REACH
PACK = 8
NET = PACK - 2
OFF = -1e30
VMEM_LIMIT = 44 * 2**20
F32, BF16 = jnp.float32, jnp.bfloat16


def split(value):
    high = value.astype(BF16)
    return high, (value - high.astype(F32)).astype(BF16)


def silu_of_double(half):
    return half + half * jnp.tanh(half)


def lane_groups(shape, size):
    return lax.broadcasted_iota(jnp.int32, shape, len(shape) - 1) // size


def fetch(sources, targets, sems):
    copies = [
        pltpu.make_async_copy(source, target, sems.at[k])
        for k, (source, target) in enumerate(zip(sources, targets))
    ]
    for copy in copies:
        copy.start()
    return copies


def arrive(copies):
    for copy in copies:
        copy.wait()


def pack_kernel(*refs):
    sources, (mid_ref, even_ref, odd_ref, par_ref) = refs[:4], refs[4:8]
    start_ref, embed_ref, dx_ref, eps_ref = refs[8:12]
    arrive(fetch(sources, refs[8:12], refs[12]))
    chans, rows, all_cols = start_ref.shape
    here, hid = embed_ref.shape
    first = lax.axis_index("tm") * (all_cols // lax.axis_size("tm")) - HALO
    shift = lax.rem(all_cols - first, all_cols)
    depth = mid_ref.shape[2]
    value = pltpu.roll(start_ref[...].reshape(chans * rows, all_cols), shift, 1)[:, :depth]
    place = lax.broadcasted_iota(jnp.int32, value.shape, 1) + first
    value = jnp.where((place >= 0) & (place < all_cols), value, 0.0)
    for c in range(chans):
        mid_ref[:, c, :] = value[c * rows : (c + 1) * rows]
    odd = lax.rem(lax.axis_index("space"), 2)
    even_ref[...] = mid_ref[pl.ds((1 - odd) * (rows - HALO), HALO)]
    odd_ref[...] = mid_ref[pl.ds(odd * (rows - HALO), HALO)]
    par_ref[:, :hid] = embed_ref[...]
    lane = lax.broadcasted_iota(jnp.int32, (1, hid), 1)
    for t in range(here):
        par_ref[t : t + 1, hid:] = jnp.where(
            lane == 0, dx_ref[t], jnp.where(lane == 1, eps_ref[t], 0.0)
        )


def column_forms(w0, w1, w2):
    even, odd = w0 * (1 / 24) + w2 * (1 / 6), w1 * (1 / 12)
    sides, middle = (w0 + w2) * (-1 / 6), w1 * (-1 / 6)
    return w0 * 0.25, sides + middle, sides - middle, even + odd, even - odd, w2


def column_points(fours):
    d0, d1, d2, d3 = (fours[:-1, k] for k in range(4))
    d4, d5 = fours[1:, 0], fours[1:, 1]
    e1, e2 = d4 - 4 * d2, d3 - 4 * d1
    e3, e4 = d4 - d2, 2 * (d3 - d1)
    return 4 * (d0 - d2) + e3, e1 + e2, e1 - e2, e3 + e4, e3 - e4, (d5 - d3) - 2 * e4


def column_outputs(m0, m1, m2, m3, m4, m5):
    s1, t1, s3, t3 = m1 + m2, m1 - m2, m3 + m4, m3 - m4
    return m0 + s1 + s3, t1 + 2 * t3, s1 + 4 * s3, t1 + 8 * t3 + m5


def weights_kernel(states, *refs):
    wi_out, wi_forms, wm_out, wo_out, bias_out, sums_out = refs[6:12]
    wi_ref, wm_ref, wo_ref, bi_ref, bm_ref, bo_ref = refs[12:18]
    arrive(fetch(refs[:6], refs[12:18], refs[18]))
    chans, hid = wi_ref.shape[2], wi_ref.shape[3]
    taps = [[wi_ref[a, b] * 0.5 for b in range(3)] for a in range(3)]
    wide_terms = [split(jnp.concatenate(taps[a], 1)) for a in range(3)]
    form_terms = [[split(form) for form in column_forms(*taps[a])] for a in range(3)]
    none = jnp.zeros((chans, 3 * hid), BF16)

    def banded(pair, terms, empty, store):
        for g in range(PACK):
            rolled = (g - 2 * pair) % PACK >= 4
            row = (g + PACK // 2) % PACK if rolled else g
            for r in range(2):
                a, low = row - 2 * pair - r, g - 2 * pair - r
                store(r, g * chans, terms[a][int(rolled)] if 0 <= a < 3 else empty)
                store(r, hid + g * chans, terms[low][0] if 0 <= low < 3 else empty)

    for pair in range(NET // 2):

        def store(r, at, value):
            wi_out[pair, at : at + chans, r * 3 * hid : (r + 1) * 3 * hid] = value

        banded(pair, wide_terms, none, store)
        for point in range(6):

            def store(r, at, value):
                wi_forms[pair, point, at : at + chans, r * hid : (r + 1) * hid] = value

            banded(pair, [t[point] for t in form_terms], none[:, :hid], store)
    for a in range(3):
        forms = column_forms(*(wm_ref[a, b].T * 0.5 for b in range(3)))
        for point, form in enumerate(forms):
            both = jnp.concatenate(split(form), 1)
            wm_out[point, 2 * a * hid : (2 * a + 1) * hid] = both
            wm_out[point, (2 * a + 1) * hid : (2 * a + 2) * hid] = both
    empty = jnp.zeros((chans, hid), F32)
    group = lane_groups((hid, hid), 2 * chans)
    for k in range(4):
        pairs = [
            [wo_ref[k - r, b] if 0 <= k - r < 3 else empty for r in range(2)] for b in range(3)
        ]
        one = jnp.concatenate(pairs[0] + pairs[1] + pairs[2] + pairs[0], 0).T
        two = jnp.concatenate([empty] * 2 + pairs[1] + pairs[2] + [empty] * 2, 0).T
        high = one.astype(BF16).astype(F32)
        one = jnp.where(group < 3, high, one - high).astype(BF16)
        both = jnp.concatenate([one, split(two)[1]], 1)
        wo_out[2 * k * hid : (2 * k + 1) * hid] = both
        wo_out[(2 * k + 1) * hid : (2 * k + 2) * hid] = both
    bias_out[0:1] = bi_ref[...].reshape(1, hid) * 0.5
    bias_out[1:2] = bm_ref[...].reshape(1, hid) * 0.5
    bias_out[2:3] = jnp.concatenate([bo_ref[...].reshape(1, chans)] * PACK, 1)
    size = sums_out.shape[0]
    source = lax.broadcasted_iota(jnp.int32, (size, size), 0)
    target = lax.broadcasted_iota(jnp.int32, (size, size), 1)
    cols = size // states
    same = (source // states) == (target % cols)
    upto = (source % states) <= (target // cols)
    sums_out[...] = jnp.where(same & upto, 1.0, 0.0).astype(BF16)


def main_kernel(tm, *refs):
    mid_ref, even_ref, odd_ref = refs[:3]
    pars = refs[3 : 3 + tm]
    bias_ref, wi_ref, wi_forms, wm_ref, wo_ref, sums_ref = refs[3 + tm : 9 + tm]
    outs = refs[9 + tm : 9 + 2 * tm]
    (
        rows_s, par_s, held_s, start_s, common_s, points_s, hid2_s, inputs_s, chunk_s,
        in_bias, mid_bias, eps_s, parts_s, turned_s, low_s,
    ) = refs[9 + 2 * tm :]
    rows, chans, depth = mid_ref.shape
    states, hid = par_s.shape[0], par_s.shape[1] // 2
    groups = points_s.shape[2] // states
    wide = 4 * groups
    cols = wide - 8
    my_tm, my_space = lax.axis_index("tm"), lax.axis_index("space")
    all_rows, all_cols = rows * lax.axis_size("space"), cols * tm
    row0, col0 = my_space * rows, my_tm * cols

    here = states // tm
    for k in range(tm):
        held_s[k] = pars[k][...]
    for k in range(tm):
        par_s[k * here : (k + 1) * here] = held_s[my_tm ^ k]

    embed = par_s[:, :hid]
    drift_x = jnp.broadcast_to(par_s[:, hid : hid + 1], (states, hid))
    drift_eps = jnp.broadcast_to(par_s[:, hid + 1 : hid + 2], (states, hid))

    def inside(first, width, limit):
        place = lax.broadcasted_iota(jnp.int32, (width, states, hid), 0)
        return (place + first >= 0) & (place + first < all_cols) & (place < limit)

    bias = bias_ref[0:1] + 0.5 * embed
    in_bias[0] = jnp.full(in_bias.shape[1:], OFF, F32)
    in_bias[1] = jnp.where(inside(col0 - 5, wide + 4, wide + 2), bias[None], OFF)
    mid_bias[0] = jnp.full(mid_bias.shape[1:], OFF, F32)
    mid_bias[1] = jnp.where(
        inside(col0 - 4, wide + 3, wide + 3),
        jnp.broadcast_to(bias_ref[1:2], (states, hid))[None],
        OFF,
    )
    reach_cols = cols + HALO
    eps_s[...] = jnp.where(inside(col0 - 3, reach_cols, reach_cols), drift_eps[None], 0.0)
    out_bias = bias_ref[2:3]

    def in_field(row):
        return jnp.where((row >= 0) & (row < all_rows), 1, 0)

    odd = lax.rem(my_space, 2) == 1
    rows_s[:HALO] = jnp.where(odd, even_ref[...], odd_ref[...])
    rows_s[HALO : HALO + rows] = mid_ref[...]
    rows_s[HALO + rows :] = jnp.where(odd, odd_ref[...], even_ref[...])

    def packed_start(first):
        return rows_s[first : first + PACK].reshape(PACK * chans, depth).T

    def left_side(pair, value, turned, low):
        group = lane_groups(value.shape, chans)
        own = (group >= 2 * pair) & (group < 2 * pair + 4)
        return jnp.concatenate([jnp.where(own, value, turned).astype(BF16), low], 1)

    def to_points(row, field):
        forms = column_points(field.reshape(groups + 1, 4, states, hid))
        for point, form in enumerate(forms):
            high, low = split(form.reshape(groups * states, hid))
            points_s[point, row, :, :hid] = high
            points_s[point, row, :, hid:] = low

    def second_hidden(count, step, row_first, col_first):
        def body(c, _):
            first = c * step
            sums = []
            for point in range(6):
                left = jnp.concatenate(
                    [
                        points_s[point, pl.ds(first + a, step)].reshape(step * groups * states, 2 * hid)
                        for a in range(3)
                    ],
                    1,
                )
                both = jnp.dot(left, wm_ref[point], preferred_element_type=F32)
                sums.append((both[:, :hid] + both[:, hid:]).reshape(step, groups, states, hid))
            field = jnp.stack(column_outputs(*sums), 2).reshape(step, wide, states, hid)
            for r in range(step):
                ok = in_field(row0 + row_first + first + r)
                value = silu_of_double(field[r] + mid_bias[ok, col_first : col_first + wide])
                high, low = split(value.reshape(wide * states, hid))
                hid2_s[first + r, :, :hid] = high
                hid2_s[first + r, :, hid:] = low
            return 0

        lax.fori_loop(0, count // step, body, 0)

    def noise(packs, width):
        units = PACK // 2 + (NET // 2) * (packs - 1)
        left = jnp.concatenate(
            [
                jnp.concatenate([hid2_s[2 * u + k] for u in range(units)], 0)
                for k in range(4)
            ],
            1,
        )
        taps = jnp.dot(left, wo_ref[...], preferred_element_type=F32)
        taps = (taps[:, :hid] + taps[:, hid:]).reshape(units, wide, states, hid)
        shape = (width, states, hid)
        group = lane_groups(shape, 2 * chans)
        one = [
            jnp.where(
                group == 1,
                taps[u, 1 : width + 1],
                jnp.where(group == 2, taps[u, 2 : width + 2], taps[u, :width]),
            )
            for u in range(units)
        ]

        def turn(value, shift):
            return pltpu.roll(value.reshape(width * states, hid), shift, 1).reshape(shape)

        lower, even = group < 2, group % 2 == 0
        values = []
        for p in range(packs):
            u0, u1, u2, u3 = one[NET // 2 * p : NET // 2 * p + 4]
            v0 = jnp.where(lower, u0, u2) + turn(jnp.where(lower, u2, u0), hid // 2)
            v1 = jnp.where(lower, u1, u3) + turn(jnp.where(lower, u3, u1), hid // 2)
            other = jnp.where(even, v1, v0)
            other = jnp.where(even, turn(other, hid - 2 * chans), turn(other, 2 * chans))
            values.append(jnp.where(even, v0, v1) + other + out_bias)
        return values

    state = lax.broadcasted_iota(jnp.int32, (1, states, hid), 1)

    def earlier(value):
        value = jnp.where(state >= 1, pltpu.roll(value, 1, 1), 0.0)
        reach = 1
        while reach < states:
            value = value + jnp.where(state >= reach, pltpu.roll(value, reach, 1), 0.0)
            reach *= 2
        return value

    packs = start_s.shape[0]
    for p in range(packs):
        start_s[p] = packed_start(NET * p)

    near = wide + 8
    for pair in range(NET // 2):
        left = []
        for p in range(packs):
            value = start_s[p, :near]
            left.append(left_side(pair, value, pltpu.roll(value, hid // 2, 1), split(value)[1]))
        taps = jnp.dot(jnp.concatenate(left, 0), wi_ref[pair], preferred_element_type=F32)
        for p in range(packs):
            for r in range(2):
                t0, t1, t2 = (
                    taps[p * near : (p + 1) * near, (3 * r + k) * hid : (3 * r + k + 1) * hid]
                    for k in range(3)
                )
                common_s[NET * p + 2 * pair + r] = (
                    t0 + pltpu.roll(t1, near - 1, 0) + pltpu.roll(t2, near - 2, 0)
                )

    def first_points(i, _):
        ok = in_field(row0 - 5 + i)
        to_points(i, silu_of_double(common_s[i, : wide + 4][:, None, :] + in_bias[ok]))
        return 0

    lax.fori_loop(0, rows + 10, first_points, 0)
    second_hidden(rows + 8, 4, -4, 0)

    packs = inputs_s.shape[0]
    value = noise(packs, reach_cols)
    group = lane_groups((1, hid), chans)
    for p in range(packs):
        start = packed_start(REACH + NET * p)[REACH : REACH + reach_cols]
        start = jnp.broadcast_to(start[:, None, :], (reach_cols, states, hid))
        row = group + (row0 - REACH + NET * p)
        keep = jnp.where((row >= 0) & (row < all_rows), 1.0, 0.0)
        drift = drift_x[None] * start + eps_s[...] * (value[p] * keep)
        total = (start + earlier(drift)).reshape(reach_cols * states, hid)
        inputs_s[p, : reach_cols * states] = total
        inputs_s[p, reach_cols * states :] = jnp.zeros(((wide - reach_cols) * states, hid), F32)

    fours = wide // 4 - 1
    for point, form in enumerate(
        zip(*(column_points(inputs_s[p].reshape(wide // 4, 4, states, hid)) for p in range(packs)))
    ):
        value = jnp.stack(form).reshape(packs * fours * states, hid)
        parts_s[point] = value
        turned_s[point] = pltpu.roll(value, hid // 2, 1)
        low_s[point] = split(value)[1]

    def second_rows(pair, _):
        products = []
        for point in range(6):
            left = left_side(pair, parts_s[point], turned_s[point], low_s[point])
            both = jnp.dot(left, wi_forms[pair, point], preferred_element_type=F32)
            products.append(both.reshape(packs, fours, states, 2 * hid))
        for p in range(packs):
            for r in range(2):
                field = jnp.stack(
                    column_outputs(*(m[p, :, :, r * hid : (r + 1) * hid] for m in products)), 1
                ).reshape(4 * fours, states, hid)
                i = NET * p + 2 * pair + r
                ok = in_field(row0 - 2 + i)
                value = silu_of_double(field + in_bias[ok, 3 : 3 + 4 * fours])
                to_points(i, jnp.concatenate([value, jnp.zeros((8, states, hid), F32)], 0))
        return 0

    lax.fori_loop(0, NET // 2, second_rows, 0)
    second_hidden(rows + 2, 5, -1, 3)

    value = noise(1, cols)[0]
    size = cols * states
    upper = inputs_s[0, REACH * states : REACH * states + size]
    lower = inputs_s[1, REACH * states : REACH * states + size]
    inputs = jnp.where(
        lane_groups((size, hid), chans) < PACK - REACH,
        pltpu.roll(upper, hid - REACH * chans, 1),
        pltpu.roll(lower, (NET - REACH) * chans, 1),
    ).reshape(cols, states, hid)
    drift = drift_x[None] * inputs + drift_eps[None] * value
    high, low = split(drift.reshape(size, hid).T)
    total = jnp.dot(high, sums_ref[...], preferred_element_type=F32) + jnp.dot(
        low, sums_ref[...], preferred_element_type=F32
    )
    start = mid_ref[...].reshape(rows * chans, depth)[:, HALO : HALO + cols]
    start = jnp.concatenate([start] * here, 1)
    width = here * cols
    for k in range(tm):
        value = start + total[:, k * width : (k + 1) * width]
        for r in range(rows):
            chunk_s[k, :, r, :] = value[r * chans : (r + 1) * chans]
    for k in range(tm):
        outs[k][...] = chunk_s[my_tm ^ k]


def join_kernel(tm, *refs):
    blocks, out_ref, held = refs[:tm], refs[tm], refs[tm + 1]
    here = out_ref.shape[0]
    cols = out_ref.shape[3] // tm
    for k in range(tm):
        held[k] = blocks[k][...]
    my_tm = lax.axis_index("tm")
    for k in range(tm):
        block = held[my_tm ^ k]
        for t in range(here):
            out_ref[t, :, :, k * cols : (k + 1) * cols] = block[:, :, t * cols : (t + 1) * cols]


def kernel_call(body, out_shape, in_specs, scratch=(), flops=0, read=0):
    vmem = pl.BlockSpec(memory_space=pltpu.VMEM)
    if isinstance(in_specs, int):
        in_specs = [vmem] * in_specs
    return pl.pallas_call(
        body,
        out_shape=out_shape,
        in_specs=in_specs,
        out_specs=jax.tree.map(lambda _: vmem, out_shape),
        scratch_shapes=list(scratch),
        compiler_params=pltpu.CompilerParams(vmem_limit_bytes=VMEM_LIMIT),
        cost_estimate=pl.CostEstimate(flops=flops, bytes_accessed=read, transcendentals=0),
    )


def in_hbm(value):
    return pltpu.with_memory_space_constraint(value, pltpu.HBM)


def on_device(start_latent, time_embed, drift_x, drift_eps, w_in, b_in, w_mid, b_mid, w_out, b_out):
    tm, space = lax.axis_size("tm"), lax.axis_size("space")
    chans, rows, all_cols = start_latent.shape
    here, hid = time_embed.shape
    states, cols = here * tm, all_cols // tm
    depth = -(-(cols + 2 * HALO) // 128) * 128
    assert rows == PACK and hid == PACK * chans
    shape, local = jax.ShapeDtypeStruct, pltpu.VMEM
    hbm = pl.BlockSpec(memory_space=pltpu.HBM)

    edge = local((HALO, chans, depth), F32)
    mid, even, odd, par = kernel_call(
        pack_kernel,
        (local((rows, chans, depth), F32), edge, edge, local((here, 2 * hid), F32)),
        [hbm] * 4,
        scratch=(
            pltpu.VMEM((chans, rows, all_cols), F32),
            pltpu.VMEM((here, hid), F32),
            pltpu.SMEM((here,), F32),
            pltpu.SMEM((here,), F32),
            pltpu.SemaphoreType.DMA((4,)),
        ),
        read=10**6,
    )(*map(in_hbm, (start_latent, time_embed, drift_x, drift_eps)))
    even = lax.ppermute(even, "space", [(i, i ^ 1) for i in range(space) if i ^ 1 < space])
    pairs = [(i, i + 1) for i in range(1, space - 1, 2)]
    odd = lax.ppermute(odd, "space", pairs + [(b, a) for a, b in pairs])
    pars = [par] + [
        lax.ppermute(par, "tm", [(i, i ^ k) for i in range(tm)]) for k in range(1, tm)
    ]

    weights = kernel_call(
        functools.partial(weights_kernel, states),
        (
            local((NET // 2, 2 * hid, 6 * hid), BF16),
            local((NET // 2, 6, 2 * hid, 2 * hid), BF16),
            local((6, 6 * hid, 2 * hid), BF16),
            local((8 * hid, 2 * hid), BF16),
            local((8, hid), F32),
            local((cols * states, cols * states), BF16),
        ),
        [hbm] * 6,
        scratch=(
            pltpu.VMEM((3, 3, chans, hid), F32),
            pltpu.VMEM((3, 3, hid, hid), F32),
            pltpu.VMEM((3, 3, chans, hid), F32),
            pltpu.VMEM((hid,), F32),
            pltpu.VMEM((hid,), F32),
            pltpu.VMEM((chans,), F32),
            pltpu.SemaphoreType.DMA((6,)),
        ),
        flops=10**7,
        read=8 * 10**6,
    )(*map(in_hbm, (w_in.transpose(0, 1, 3, 2), w_mid, w_out, b_in, b_mid, b_out)))
    wi, wi_forms, wm, wo, bias, sums = weights

    groups = (cols + 8) // 4
    wide = 4 * groups
    width = here * cols
    parts = (rows + HALO - 2) // NET * (groups - 1) * states
    chunks = kernel_call(
        functools.partial(main_kernel, tm),
        tuple(local((chans, rows, width), F32) for _ in range(tm)),
        9 + tm,
        scratch=(
            pltpu.VMEM((rows + 2 * HALO, chans, depth), F32),
            pltpu.VMEM((states, 2 * hid), F32),
            pltpu.VMEM((tm, here, 2 * hid), F32),
            pltpu.VMEM(((rows + 2 * HALO - 2) // NET, depth, hid), F32),
            pltpu.VMEM((rows + 10, wide + 8, hid), F32),
            pltpu.VMEM((6, rows + 10, groups * states, 2 * hid), BF16),
            pltpu.VMEM((rows + 8, wide * states, 2 * hid), BF16),
            pltpu.VMEM(((rows + HALO - 2) // NET, wide * states, hid), F32),
            pltpu.VMEM((tm, chans, rows, width), F32),
            pltpu.VMEM((2, wide + 4, states, hid), F32),
            pltpu.VMEM((2, wide + 3, states, hid), F32),
            pltpu.VMEM((cols + HALO, states, hid), F32),
            *(pltpu.VMEM((6, parts, hid), kind) for kind in (F32, F32, BF16)),
        ),
        flops=10**10,
        read=8 * 10**6,
    )(mid, even, odd, *pars, bias, wi, wi_forms, wm, wo, sums)

    blocks = [chunks[0]] + [
        lax.ppermute(chunks[k], "tm", [(i, i ^ k) for i in range(tm)]) for k in range(1, tm)
    ]
    return kernel_call(
        functools.partial(join_kernel, tm),
        shape((here, chans, rows, all_cols), F32),
        tm,
        scratch=(pltpu.VMEM((tm, chans, rows, width), F32),),
        read=10**6,
    )(*blocks)


def solution(mesh):
    in_specs = (
        P("group", "space", None),
        P("tm", None),
        P("tm"),
        P("tm"),
        P(),
        P(),
        P(),
        P(),
        P(),
        P(),
    )
    out_specs = P("tm", "group", "space", None)
    return jax.shard_map(
        on_device, mesh=mesh, in_specs=in_specs, out_specs=out_specs, check_vma=False
    )
```

```python
import functools
import jax
import jax.numpy as jnp
from jax import lax
from jax.experimental import pallas as pl
from jax.experimental.pallas import tpu as pltpu
from jax.sharding import PartitionSpec as P

REACH = 3
HALO = 2 * REACH
PACK = 8
PIECE = 2
NET = PACK - 2
OFF = -1e30
VMEM_LIMIT = 44 * 2**20
F32, BF16 = jnp.float32, jnp.bfloat16


def split(value):
    high = value.astype(BF16)
    return high, (value - high.astype(F32)).astype(BF16)


def silu_of_double(half):
    return half + half * jnp.tanh(half)


def lane_groups(shape, size):
    return lax.broadcasted_iota(jnp.int32, shape, len(shape) - 1) // size


def fetch(sources, targets, sems):
    copies = [
        pltpu.make_async_copy(source, target, sems.at[k])
        for k, (source, target) in enumerate(zip(sources, targets))
    ]
    for copy in copies:
        copy.start()
    return copies


def arrive(copies):
    for copy in copies:
        copy.wait()


def pack_kernel(*refs):
    sources, (mid_ref, even_ref, odd_ref, par_ref) = refs[:4], refs[4:8]
    start_ref, embed_ref, dx_ref, eps_ref = refs[8:12]
    arrive(fetch(sources, refs[8:12], refs[12]))
    chans, rows, all_cols = start_ref.shape
    here, hid = embed_ref.shape
    first = lax.axis_index("tm") * (all_cols // lax.axis_size("tm")) - HALO
    shift = lax.rem(all_cols - first, all_cols)
    depth = mid_ref.shape[2]
    value = pltpu.roll(start_ref[...].reshape(chans * rows, all_cols), shift, 1)[:, :depth]
    place = lax.broadcasted_iota(jnp.int32, value.shape, 1) + first
    value = jnp.where((place >= 0) & (place < all_cols), value, 0.0)
    for c in range(chans):
        mid_ref[:, c, :] = value[c * rows : (c + 1) * rows]
    odd = lax.rem(lax.axis_index("space"), 2)
    even_ref[...] = mid_ref[pl.ds((1 - odd) * (rows - HALO), HALO)]
    odd_ref[...] = mid_ref[pl.ds(odd * (rows - HALO), HALO)]
    par_ref[:, :hid] = embed_ref[...]
    lane = lax.broadcasted_iota(jnp.int32, (1, hid), 1)
    for t in range(here):
        par_ref[t : t + 1, hid:] = jnp.where(
            lane == 0, dx_ref[t], jnp.where(lane == 1, eps_ref[t], 0.0)
        )


def column_forms(w0, w1, w2):
    even, odd = w0 * (1 / 24) + w2 * (1 / 6), w1 * (1 / 12)
    sides, middle = (w0 + w2) * (-1 / 6), w1 * (-1 / 6)
    return w0 * 0.25, sides + middle, sides - middle, even + odd, even - odd, w2


def column_points(fours, behind):
    d0, d1, d2, d3 = (fours[:, k] for k in range(4))
    d4, d5 = (jnp.concatenate([fours[1:, k], behind[:1, k]], 0) for k in range(2))
    e1, e2 = d4 - 4 * d2, d3 - 4 * d1
    e3, e4 = d4 - d2, 2 * (d3 - d1)
    return 4 * (d0 - d2) + e3, e1 + e2, e1 - e2, e3 + e4, e3 - e4, (d5 - d3) - 2 * e4


def column_outputs(m0, m1, m2, m3, m4, m5):
    s1, t1, s3, t3 = m1 + m2, m1 - m2, m3 + m4, m3 - m4
    return m0 + s1 + s3, t1 + 2 * t3, s1 + 4 * s3, t1 + 8 * t3 + m5


def weights_kernel(states, *refs):
    wi_out, wi_forms, wm_out, wo_out, bias_out, sums_out = refs[6:12]
    wi_ref, wm_ref, wo_ref, bi_ref, bm_ref, bo_ref = refs[12:18]
    arrive(fetch(refs[:6], refs[12:18], refs[18]))
    chans, hid = wi_ref.shape[2], wi_ref.shape[3]
    taps = [[wi_ref[a, b] * 0.5 for b in range(3)] for a in range(3)]
    wide_terms = [split(jnp.concatenate(taps[a], 1)) for a in range(3)]
    form_terms = [[split(form) for form in column_forms(*taps[a])] for a in range(3)]
    none = jnp.zeros((chans, 3 * hid), BF16)

    def banded(pair, terms, empty, store):
        for g in range(PACK):
            rolled = (g - 2 * pair) % PACK >= 4
            row = (g + PACK // 2) % PACK if rolled else g
            for r in range(2):
                a, low = row - 2 * pair - r, g - 2 * pair - r
                store(r, g * chans, terms[a][int(rolled)] if 0 <= a < 3 else empty)
                store(r, hid + g * chans, terms[low][0] if 0 <= low < 3 else empty)

    for pair in range(NET // 2):

        def store(r, at, value):
            wi_out[pair, at : at + chans, r * 3 * hid : (r + 1) * 3 * hid] = value

        banded(pair, wide_terms, none, store)
        for point in range(6):

            def store(r, at, value):
                wi_forms[pair, point, at : at + chans, r * hid : (r + 1) * hid] = value

            banded(pair, [t[point] for t in form_terms], none[:, :hid], store)
    for a in range(3):
        forms = column_forms(*(wm_ref[a, b].T * 0.5 for b in range(3)))
        for point, form in enumerate(forms):
            both = jnp.concatenate(split(form), 1)
            wm_out[point, 2 * a * hid : (2 * a + 1) * hid] = both
            wm_out[point, (2 * a + 1) * hid : (2 * a + 2) * hid] = both
    empty = jnp.zeros((chans, hid), F32)
    group = lane_groups((hid, hid), 2 * chans)
    for k in range(4):
        pairs = [
            [wo_ref[k - r, b] if 0 <= k - r < 3 else empty for r in range(2)] for b in range(3)
        ]
        one = jnp.concatenate(pairs[0] + pairs[1] + pairs[2] + pairs[0], 0).T
        two = jnp.concatenate([empty] * 2 + pairs[1] + pairs[2] + [empty] * 2, 0).T
        high = one.astype(BF16).astype(F32)
        one = jnp.where(group < 3, high, one - high).astype(BF16)
        both = jnp.concatenate([one, split(two)[1]], 1)
        wo_out[2 * k * hid : (2 * k + 1) * hid] = both
        wo_out[(2 * k + 1) * hid : (2 * k + 2) * hid] = both
    bias_out[0:1] = bi_ref[...].reshape(1, hid) * 0.5
    bias_out[1:2] = bm_ref[...].reshape(1, hid) * 0.5
    bias_out[2:3] = jnp.concatenate([bo_ref[...].reshape(1, chans)] * PACK, 1)
    size = sums_out.shape[0]
    source = lax.broadcasted_iota(jnp.int32, (size, size), 0)
    target = lax.broadcasted_iota(jnp.int32, (size, size), 1)
    cols = size // states
    same = (source // states) == (target % cols)
    upto = (source % states) <= (target // cols)
    sums_out[...] = jnp.where(same & upto, 1.0, 0.0).astype(BF16)


def main_kernel(tm, *refs):
    mid_ref, even_ref, odd_ref = refs[:3]
    pars = refs[3 : 3 + tm]
    bias_ref, wi_ref, wi_forms, wm_ref, wo_ref, sums_ref = refs[3 + tm : 9 + tm]
    outs = refs[9 + tm : 9 + 2 * tm]
    (
        rows_s, par_s, held_s, start_s, common_s, points_s, hid2_s, inputs_s, chunk_s,
        in_bias, mid_bias, eps_s, parts_s, turned_s, low_s,
    ) = refs[9 + 2 * tm :]
    rows, chans, depth = mid_ref.shape
    states, hid = par_s.shape[0], par_s.shape[1] // 2
    groups = points_s.shape[2] // states
    wide = 4 * groups
    cols = wide - 8
    my_tm, my_space = lax.axis_index("tm"), lax.axis_index("space")
    all_rows, all_cols = rows * lax.axis_size("space"), cols * tm
    row0, col0 = my_space * rows, my_tm * cols

    here = states // tm
    for k in range(tm):
        held_s[k] = pars[k][...]
    for k in range(tm):
        par_s[k * here : (k + 1) * here] = held_s[my_tm ^ k]

    embed = par_s[:, :hid]
    drift_x = jnp.broadcast_to(par_s[:, hid : hid + 1], (states, hid))
    drift_eps = jnp.broadcast_to(par_s[:, hid + 1 : hid + 2], (states, hid))

    def inside(first, width, limit):
        place = lax.broadcasted_iota(jnp.int32, (width, states, hid), 0)
        return (place + first >= 0) & (place + first < all_cols) & (place < limit)

    bias = bias_ref[0:1] + 0.5 * embed
    in_bias[0] = jnp.full(in_bias.shape[1:], OFF, F32)
    in_bias[1] = jnp.where(inside(col0 - 5, wide + 4, wide + 2), bias[None], OFF)
    mid_bias[0] = jnp.full(mid_bias.shape[1:], OFF, F32)
    mid_bias[1] = jnp.where(
        inside(col0 - 4, wide + 3, wide + 3),
        jnp.broadcast_to(bias_ref[1:2], (states, hid))[None],
        OFF,
    )
    reach_cols = cols + HALO
    eps_s[...] = jnp.where(inside(col0 - 3, reach_cols, reach_cols), drift_eps[None], 0.0)
    out_bias = bias_ref[2:3]

    def in_field(row):
        return jnp.where((row >= 0) & (row < all_rows), 1, 0)

    odd = lax.rem(my_space, 2) == 1
    rows_s[:HALO] = jnp.where(odd, even_ref[...], odd_ref[...])
    rows_s[HALO : HALO + rows] = mid_ref[...]
    rows_s[HALO + rows :] = jnp.where(odd, odd_ref[...], even_ref[...])

    def packed_start(first):
        return rows_s[first : first + PACK].reshape(PACK * chans, depth).T

    def left_side(pair, value, turned, low):
        group = lane_groups(value.shape, chans)
        own = (group >= 2 * pair) & (group < 2 * pair + 4)
        return jnp.concatenate([jnp.where(own, value, turned).astype(BF16), low], 1)

    def pieces(count):
        return [(first, min(first + PIECE, count)) for first in range(0, count, PIECE)]

    def to_points(row, field, behind):
        for first, last in reversed(pieces(groups)):
            fours = field(first, last)
            for point, form in enumerate(column_points(fours, behind)):
                high, low = split(form.reshape((last - first) * states, hid))
                points_s[point, row, first * states : last * states, :hid] = high
                points_s[point, row, first * states : last * states, hid:] = low
            behind = fours

    def second_hidden(chosen, row_first, col_first, beside=()):
        beside = list(beside)
        step = len(chosen)
        sums = []
        for point in range(6):
            left = jnp.concatenate(
                [
                    jnp.concatenate([points_s[point, i + a] for i in chosen], 0)
                    for a in range(3)
                ],
                1,
            )
            both = jnp.dot(left, wm_ref[point], preferred_element_type=F32)
            sums.append(both.reshape(step, groups, states, 2 * hid))
            if beside:
                beside.pop(0)()
        for r, i in enumerate(chosen):
            ok = in_field(row0 + row_first + i)
            for first, last in pieces(groups):
                parts = [m[r, first:last] for m in sums]
                parts = [m[:, :, :hid] + m[:, :, hid:] for m in parts]
                size = 4 * (last - first)
                field = jnp.stack(column_outputs(*parts), 1).reshape(size, states, hid)
                bias = mid_bias[ok, col_first + 4 * first : col_first + 4 * last]
                high, low = split(silu_of_double(field + bias).reshape(size * states, hid))
                place = slice(4 * first * states, 4 * last * states)
                hid2_s[i, place, :hid] = high
                hid2_s[i, place, hid:] = low

    def noise(packs, width):
        units = PACK // 2 + (NET // 2) * (packs - 1)
        left = jnp.concatenate(
            [
                jnp.concatenate([hid2_s[2 * u + k] for u in range(units)], 0)
                for k in range(4)
            ],
            1,
        )
        taps = jnp.dot(left, wo_ref[...], preferred_element_type=F32)
        taps = (taps[:, :hid] + taps[:, hid:]).reshape(units, wide, states, hid)
        shape = (width, states, hid)
        group = lane_groups(shape, 2 * chans)
        one = [
            jnp.where(
                group == 1,
                taps[u, 1 : width + 1],
                jnp.where(group == 2, taps[u, 2 : width + 2], taps[u, :width]),
            )
            for u in range(units)
        ]

        def turn(value, shift):
            return pltpu.roll(value.reshape(width * states, hid), shift, 1).reshape(shape)

        lower, even = group < 2, group % 2 == 0
        values = []
        for p in range(packs):
            u0, u1, u2, u3 = one[NET // 2 * p : NET // 2 * p + 4]
            v0 = jnp.where(lower, u0, u2) + turn(jnp.where(lower, u2, u0), hid // 2)
            v1 = jnp.where(lower, u1, u3) + turn(jnp.where(lower, u3, u1), hid // 2)
            other = jnp.where(even, v1, v0)
            other = jnp.where(even, turn(other, hid - 2 * chans), turn(other, 2 * chans))
            values.append(jnp.where(even, v0, v1) + other + out_bias)
        return values

    state = lax.broadcasted_iota(jnp.int32, (1, states, hid), 1)

    def earlier(value):
        value = jnp.where(state >= 1, pltpu.roll(value, 1, 1), 0.0)
        reach = 1
        while reach < states:
            value = value + jnp.where(state >= reach, pltpu.roll(value, reach, 1), 0.0)
            reach *= 2
        return value

    packs = start_s.shape[0]
    for p in range(packs):
        start_s[p] = packed_start(NET * p)

    near = wide + 8
    for pair in range(NET // 2):
        left = []
        for p in range(packs):
            value = start_s[p, :near]
            left.append(left_side(pair, value, pltpu.roll(value, hid // 2, 1), split(value)[1]))
        taps = jnp.dot(jnp.concatenate(left, 0), wi_ref[pair], preferred_element_type=F32)
        for p in range(packs):
            for r in range(2):
                t0, t1, t2 = (
                    taps[p * near : (p + 1) * near, (3 * r + k) * hid : (3 * r + k + 1) * hid]
                    for k in range(3)
                )
                common_s[NET * p + 2 * pair + r] = (
                    t0 + pltpu.roll(t1, near - 1, 0) + pltpu.roll(t2, near - 2, 0)
                )

    def first_points(i):
        ok = in_field(row0 - 5 + i)

        def field(first, last):
            place = slice(4 * first, 4 * last)
            value = silu_of_double(common_s[i, place][:, None, :] + in_bias[ok, place])
            return value.reshape(last - first, 4, states, hid)

        to_points(i, field, field(groups, groups + 1))

    step = 4
    calls = [functools.partial(first_points, i) for i in range(rows + 10)]
    for call in calls[: step + 2]:
        call()
    for first in range(0, rows + 8, step):
        ahead = first + step + 2
        second_hidden(range(first, first + step), -4, 0, calls[ahead : ahead + step])

    packs = inputs_s.shape[0]
    value = noise(packs, reach_cols)
    group = lane_groups((1, hid), chans)
    for p in range(packs):
        start = packed_start(REACH + NET * p)[REACH : REACH + reach_cols]
        start = jnp.broadcast_to(start[:, None, :], (reach_cols, states, hid))
        row = group + (row0 - REACH + NET * p)
        keep = jnp.where((row >= 0) & (row < all_rows), 1.0, 0.0)
        drift = drift_x[None] * start + eps_s[...] * (value[p] * keep)
        total = (start + earlier(drift)).reshape(reach_cols * states, hid)
        inputs_s[p, : reach_cols * states] = total
        inputs_s[p, reach_cols * states :] = jnp.zeros(((wide - reach_cols) * states, hid), F32)

    fours = wide // 4 - 1
    packed = [inputs_s[p].reshape(groups, 4, states, hid) for p in range(packs)]
    packed = [column_points(v[:fours], v[fours:]) for v in packed]
    for point, form in enumerate(zip(*packed)):
        value = jnp.stack(form).reshape(packs * fours * states, hid)
        parts_s[point] = value
        turned_s[point] = pltpu.roll(value, hid // 2, 1)
        low_s[point] = split(value)[1]

    def second_rows(pair):
        products = []
        for point in range(6):
            left = left_side(pair, parts_s[point], turned_s[point], low_s[point])
            both = jnp.dot(left, wi_forms[pair, point], preferred_element_type=F32)
            products.append(both.reshape(packs, fours, states, 2 * hid))
        for p in range(packs):
            for r in range(2):
                i = NET * p + 2 * pair + r
                ok = in_field(row0 - 2 + i)

                def field(first, last, p=p, r=r, ok=ok):
                    last = min(last, fours)
                    parts = [m[p, first:last, :, r * hid : (r + 1) * hid] for m in products]
                    value = jnp.stack(column_outputs(*parts), 1)
                    bias = in_bias[ok, 3 + 4 * first : 3 + 4 * last].reshape(value.shape)
                    value = silu_of_double(value + bias)
                    return jnp.concatenate([value, none], 0) if last == fours else value

                none = jnp.zeros((1, 4, states, hid), F32)
                to_points(i, field, none)

    calls = [functools.partial(second_rows, pair) for pair in range(NET // 2)]
    calls[0]()
    calls[1]()
    second_hidden([0, 1, NET, NET + 1], -1, 3, calls[2:])
    second_hidden([2, 3, 4, 5, NET + 2, NET + 3], -1, 3)

    value = noise(1, cols)[0]
    size = cols * states
    upper = inputs_s[0, REACH * states : REACH * states + size]
    lower = inputs_s[1, REACH * states : REACH * states + size]
    inputs = jnp.where(
        lane_groups((size, hid), chans) < PACK - REACH,
        pltpu.roll(upper, hid - REACH * chans, 1),
        pltpu.roll(lower, (NET - REACH) * chans, 1),
    ).reshape(cols, states, hid)
    drift = drift_x[None] * inputs + drift_eps[None] * value
    high, low = split(drift.reshape(size, hid).T)
    total = jnp.dot(high, sums_ref[...], preferred_element_type=F32) + jnp.dot(
        low, sums_ref[...], preferred_element_type=F32
    )
    start = mid_ref[...].reshape(rows * chans, depth)[:, HALO : HALO + cols]
    start = jnp.concatenate([start] * here, 1)
    width = here * cols
    for k in range(tm):
        value = start + total[:, k * width : (k + 1) * width]
        for r in range(rows):
            chunk_s[k, :, r, :] = value[r * chans : (r + 1) * chans]
    for k in range(tm):
        outs[k][...] = chunk_s[my_tm ^ k]


def join_kernel(tm, *refs):
    blocks, out_ref, held = refs[:tm], refs[tm], refs[tm + 1]
    here = out_ref.shape[0]
    cols = out_ref.shape[3] // tm
    for k in range(tm):
        held[k] = blocks[k][...]
    my_tm = lax.axis_index("tm")
    for k in range(tm):
        block = held[my_tm ^ k]
        for t in range(here):
            out_ref[t, :, :, k * cols : (k + 1) * cols] = block[:, :, t * cols : (t + 1) * cols]


def kernel_call(body, out_shape, in_specs, scratch=(), flops=0, read=0):
    vmem = pl.BlockSpec(memory_space=pltpu.VMEM)
    if isinstance(in_specs, int):
        in_specs = [vmem] * in_specs
    return pl.pallas_call(
        body,
        out_shape=out_shape,
        in_specs=in_specs,
        out_specs=jax.tree.map(lambda _: vmem, out_shape),
        scratch_shapes=list(scratch),
        compiler_params=pltpu.CompilerParams(vmem_limit_bytes=VMEM_LIMIT),
        cost_estimate=pl.CostEstimate(flops=flops, bytes_accessed=read, transcendentals=0),
    )


def in_hbm(value):
    return pltpu.with_memory_space_constraint(value, pltpu.HBM)


def on_device(start_latent, time_embed, drift_x, drift_eps, w_in, b_in, w_mid, b_mid, w_out, b_out):
    tm, space = lax.axis_size("tm"), lax.axis_size("space")
    chans, rows, all_cols = start_latent.shape
    here, hid = time_embed.shape
    states, cols = here * tm, all_cols // tm
    depth = -(-(cols + 2 * HALO) // 128) * 128
    assert rows == PACK and hid == PACK * chans
    shape, local = jax.ShapeDtypeStruct, pltpu.VMEM
    hbm = pl.BlockSpec(memory_space=pltpu.HBM)

    edge = local((HALO, chans, depth), F32)
    mid, even, odd, par = kernel_call(
        pack_kernel,
        (local((rows, chans, depth), F32), edge, edge, local((here, 2 * hid), F32)),
        [hbm] * 4,
        scratch=(
            pltpu.VMEM((chans, rows, all_cols), F32),
            pltpu.VMEM((here, hid), F32),
            pltpu.SMEM((here,), F32),
            pltpu.SMEM((here,), F32),
            pltpu.SemaphoreType.DMA((4,)),
        ),
        read=10**6,
    )(*map(in_hbm, (start_latent, time_embed, drift_x, drift_eps)))
    even = lax.ppermute(even, "space", [(i, i ^ 1) for i in range(space) if i ^ 1 < space])
    pairs = [(i, i + 1) for i in range(1, space - 1, 2)]
    odd = lax.ppermute(odd, "space", pairs + [(b, a) for a, b in pairs])
    pars = [par] + [
        lax.ppermute(par, "tm", [(i, i ^ k) for i in range(tm)]) for k in range(1, tm)
    ]

    weights = kernel_call(
        functools.partial(weights_kernel, states),
        (
            local((NET // 2, 2 * hid, 6 * hid), BF16),
            local((NET // 2, 6, 2 * hid, 2 * hid), BF16),
            local((6, 6 * hid, 2 * hid), BF16),
            local((8 * hid, 2 * hid), BF16),
            local((8, hid), F32),
            local((cols * states, cols * states), BF16),
        ),
        [hbm] * 6,
        scratch=(
            pltpu.VMEM((3, 3, chans, hid), F32),
            pltpu.VMEM((3, 3, hid, hid), F32),
            pltpu.VMEM((3, 3, chans, hid), F32),
            pltpu.VMEM((hid,), F32),
            pltpu.VMEM((hid,), F32),
            pltpu.VMEM((chans,), F32),
            pltpu.SemaphoreType.DMA((6,)),
        ),
        flops=10**7,
        read=8 * 10**6,
    )(*map(in_hbm, (w_in.transpose(0, 1, 3, 2), w_mid, w_out, b_in, b_mid, b_out)))
    wi, wi_forms, wm, wo, bias, sums = weights

    groups = (cols + 8) // 4
    wide = 4 * groups
    width = here * cols
    parts = (rows + HALO - 2) // NET * (groups - 1) * states
    chunks = kernel_call(
        functools.partial(main_kernel, tm),
        tuple(local((chans, rows, width), F32) for _ in range(tm)),
        9 + tm,
        scratch=(
            pltpu.VMEM((rows + 2 * HALO, chans, depth), F32),
            pltpu.VMEM((states, 2 * hid), F32),
            pltpu.VMEM((tm, here, 2 * hid), F32),
            pltpu.VMEM(((rows + 2 * HALO - 2) // NET, depth, hid), F32),
            pltpu.VMEM((rows + 10, wide + 8, hid), F32),
            pltpu.VMEM((6, rows + 10, groups * states, 2 * hid), BF16),
            pltpu.VMEM((rows + 8, wide * states, 2 * hid), BF16),
            pltpu.VMEM(((rows + HALO - 2) // NET, wide * states, hid), F32),
            pltpu.VMEM((tm, chans, rows, width), F32),
            pltpu.VMEM((2, wide + 4, states, hid), F32),
            pltpu.VMEM((2, wide + 3, states, hid), F32),
            pltpu.VMEM((cols + HALO, states, hid), F32),
            *(pltpu.VMEM((6, parts, hid), kind) for kind in (F32, F32, BF16)),
        ),
        flops=10**10,
        read=8 * 10**6,
    )(mid, even, odd, *pars, bias, wi, wi_forms, wm, wo, sums)

    blocks = [chunks[0]] + [
        lax.ppermute(chunks[k], "tm", [(i, i ^ k) for i in range(tm)]) for k in range(1, tm)
    ]
    return kernel_call(
        functools.partial(join_kernel, tm),
        shape((here, chans, rows, all_cols), F32),
        tm,
        scratch=(pltpu.VMEM((tm, chans, rows, width), F32),),
        read=10**6,
    )(*blocks)


def solution(mesh):
    in_specs = (
        P("group", "space", None),
        P("tm", None),
        P("tm"),
        P("tm"),
        P(),
        P(),
        P(),
        P(),
        P(),
        P(),
    )
    out_specs = P("tm", "group", "space", None)
    return jax.shard_map(
        on_device, mesh=mesh, in_specs=in_specs, out_specs=out_specs, check_vma=False
    )
```

```python
import functools
import jax
import jax.numpy as jnp
from jax import lax
from jax.experimental import pallas as pl
from jax.experimental.pallas import tpu as pltpu
from jax.sharding import PartitionSpec as P

REACH = 3
HALO = 2 * REACH
PACK = 8
PIECE = 2
FEW = 4
NET = PACK - 2
OFF = -1e30
VMEM_LIMIT = 44 * 2**20
F32, BF16 = jnp.float32, jnp.bfloat16


def split(value):
    high = value.astype(BF16)
    return high, (value - high.astype(F32)).astype(BF16)


def silu_of_double(half):
    return half + half * jnp.tanh(half)


def lane_groups(shape, size):
    return lax.broadcasted_iota(jnp.int32, shape, len(shape) - 1) // size


def fetch(sources, targets, sems):
    copies = [
        pltpu.make_async_copy(source, target, sems.at[k])
        for k, (source, target) in enumerate(zip(sources, targets))
    ]
    for copy in copies:
        copy.start()
    return copies


def arrive(copies):
    for copy in copies:
        copy.wait()


def pack_kernel(*refs):
    sources, (mid_ref, even_ref, odd_ref, par_ref) = refs[:4], refs[4:8]
    start_ref, embed_ref, dx_ref, eps_ref = refs[8:12]
    arrive(fetch(sources, refs[8:12], refs[12]))
    chans, rows, all_cols = start_ref.shape
    here, hid = embed_ref.shape
    first = lax.axis_index("tm") * (all_cols // lax.axis_size("tm")) - HALO
    shift = lax.rem(all_cols - first, all_cols)
    depth = mid_ref.shape[2]
    value = pltpu.roll(start_ref[...].reshape(chans * rows, all_cols), shift, 1)[:, :depth]
    place = lax.broadcasted_iota(jnp.int32, value.shape, 1) + first
    value = jnp.where((place >= 0) & (place < all_cols), value, 0.0)
    for c in range(chans):
        mid_ref[:, c, :] = value[c * rows : (c + 1) * rows]
    odd = lax.rem(lax.axis_index("space"), 2)
    even_ref[...] = mid_ref[pl.ds((1 - odd) * (rows - HALO), HALO)]
    odd_ref[...] = mid_ref[pl.ds(odd * (rows - HALO), HALO)]
    par_ref[:, :hid] = embed_ref[...]
    lane = lax.broadcasted_iota(jnp.int32, (1, hid), 1)
    for t in range(here):
        par_ref[t : t + 1, hid:] = jnp.where(
            lane == 0, dx_ref[t], jnp.where(lane == 1, eps_ref[t], 0.0)
        )


def column_forms(w0, w1, w2):
    even, odd = w0 * (1 / 24) + w2 * (1 / 6), w1 * (1 / 12)
    sides, middle = (w0 + w2) * (-1 / 6), w1 * (-1 / 6)
    return w0 * 0.25, sides + middle, sides - middle, even + odd, even - odd, w2


def column_points(fours, behind):
    d0, d1, d2, d3 = (fours[:, k] for k in range(4))
    d4, d5 = (jnp.concatenate([fours[1:, k], behind[:1, k]], 0) for k in range(2))
    e1, e2 = d4 - 4 * d2, d3 - 4 * d1
    e3, e4 = d4 - d2, 2 * (d3 - d1)
    return 4 * (d0 - d2) + e3, e1 + e2, e1 - e2, e3 + e4, e3 - e4, (d5 - d3) - 2 * e4


def column_outputs(m0, m1, m2, m3, m4, m5):
    s1, t1, s3, t3 = m1 + m2, m1 - m2, m3 + m4, m3 - m4
    return m0 + s1 + s3, t1 + 2 * t3, s1 + 4 * s3, t1 + 8 * t3 + m5


def weights_kernel(states, *refs):
    wi_out, wi_forms, wm_out, wo_out, bias_out, sums_out = refs[6:12]
    wi_ref, wm_ref, wo_ref, bi_ref, bm_ref, bo_ref = refs[12:18]
    arrive(fetch(refs[:6], refs[12:18], refs[18]))
    chans, hid = wi_ref.shape[2], wi_ref.shape[3]
    taps = [[wi_ref[a, b] * 0.5 for b in range(3)] for a in range(3)]
    wide_terms = [split(jnp.concatenate(taps[a], 1)) for a in range(3)]
    form_terms = [[split(form) for form in column_forms(*taps[a])] for a in range(3)]
    none = jnp.zeros((chans, 3 * hid), BF16)

    def banded(pair, terms, empty, store):
        for g in range(PACK):
            rolled = (g - 2 * pair) % PACK >= 4
            row = (g + PACK // 2) % PACK if rolled else g
            for r in range(2):
                a, low = row - 2 * pair - r, g - 2 * pair - r
                store(r, g * chans, terms[a][int(rolled)] if 0 <= a < 3 else empty)
                store(r, hid + g * chans, terms[low][0] if 0 <= low < 3 else empty)

    for pair in range(NET // 2):

        def store(r, at, value):
            wi_out[pair, at : at + chans, r * 3 * hid : (r + 1) * 3 * hid] = value

        banded(pair, wide_terms, none, store)
        for point in range(6):

            def store(r, at, value):
                wi_forms[pair, point, at : at + chans, r * hid : (r + 1) * hid] = value

            banded(pair, [t[point] for t in form_terms], none[:, :hid], store)
    for a in range(3):
        forms = column_forms(*(wm_ref[a, b].T * 0.5 for b in range(3)))
        for point, form in enumerate(forms):
            both = jnp.concatenate(split(form), 1)
            wm_out[point, 2 * a * hid : (2 * a + 1) * hid] = both
            wm_out[point, (2 * a + 1) * hid : (2 * a + 2) * hid] = both
    empty = jnp.zeros((chans, hid), F32)
    group = lane_groups((hid, hid), 2 * chans)
    for k in range(4):
        pairs = [
            [wo_ref[k - r, b] if 0 <= k - r < 3 else empty for r in range(2)] for b in range(3)
        ]
        one = jnp.concatenate(pairs[0] + pairs[1] + pairs[2] + pairs[0], 0).T
        two = jnp.concatenate([empty] * 2 + pairs[1] + pairs[2] + [empty] * 2, 0).T
        high = one.astype(BF16).astype(F32)
        one = jnp.where(group < 3, high, one - high).astype(BF16)
        both = jnp.concatenate([one, split(two)[1]], 1)
        wo_out[2 * k * hid : (2 * k + 1) * hid] = both
        wo_out[(2 * k + 1) * hid : (2 * k + 2) * hid] = both
    bias_out[0:1] = bi_ref[...].reshape(1, hid) * 0.5
    bias_out[1:2] = bm_ref[...].reshape(1, hid) * 0.5
    bias_out[2:3] = jnp.concatenate([bo_ref[...].reshape(1, chans)] * PACK, 1)
    size = sums_out.shape[0]
    source = lax.broadcasted_iota(jnp.int32, (size, size), 0)
    target = lax.broadcasted_iota(jnp.int32, (size, size), 1)
    cols = size // states
    same = (source // states) == (target % cols)
    upto = (source % states) <= (target // cols)
    sums_out[...] = jnp.where(same & upto, 1.0, 0.0).astype(BF16)


def main_kernel(tm, *refs):
    mid_ref, even_ref, odd_ref = refs[:3]
    pars = refs[3 : 3 + tm]
    bias_ref, wi_ref, wi_forms, wm_ref, wo_ref, sums_ref = refs[3 + tm : 9 + tm]
    outs = refs[9 + tm : 9 + 2 * tm]
    (
        rows_s, par_s, held_s, start_s, common_s, points_s, hid2_s, inputs_s, chunk_s,
        in_bias, mid_bias, eps_s, parts_s, turned_s, low_s, last_s,
    ) = refs[9 + 2 * tm :]
    rows, chans, depth = mid_ref.shape
    states, hid = par_s.shape[0], par_s.shape[1] // 2
    groups = points_s.shape[2] // states
    wide = 4 * groups
    cols = wide - 8
    my_tm, my_space = lax.axis_index("tm"), lax.axis_index("space")
    all_rows, all_cols = rows * lax.axis_size("space"), cols * tm
    row0, col0 = my_space * rows, my_tm * cols

    here = states // tm
    for k in range(tm):
        held_s[k] = pars[k][...]
    for k in range(tm):
        par_s[k * here : (k + 1) * here] = held_s[my_tm ^ k]

    embed = par_s[:, :hid]
    drift_x = jnp.broadcast_to(par_s[:, hid : hid + 1], (states, hid))
    drift_eps = jnp.broadcast_to(par_s[:, hid + 1 : hid + 2], (states, hid))

    def inside(first, width, limit):
        place = lax.broadcasted_iota(jnp.int32, (width, states, hid), 0)
        return (place + first >= 0) & (place + first < all_cols) & (place < limit)

    bias = bias_ref[0:1] + 0.5 * embed
    in_bias[0] = jnp.full(in_bias.shape[1:], OFF, F32)
    in_bias[1] = jnp.where(inside(col0 - 5, wide + 4, wide + 2), bias[None], OFF)
    mid_bias[0] = jnp.full(mid_bias.shape[1:], OFF, F32)
    mid_bias[1] = jnp.where(
        inside(col0 - 4, wide + 3, wide + 3),
        jnp.broadcast_to(bias_ref[1:2], (states, hid))[None],
        OFF,
    )
    reach_cols = cols + HALO
    eps_s[...] = jnp.where(inside(col0 - 3, reach_cols, reach_cols), drift_eps[None], 0.0)
    out_bias = bias_ref[2:3]

    def in_field(row):
        return jnp.where((row >= 0) & (row < all_rows), 1, 0)

    odd = lax.rem(my_space, 2) == 1
    rows_s[:HALO] = jnp.where(odd, even_ref[...], odd_ref[...])
    rows_s[HALO : HALO + rows] = mid_ref[...]
    rows_s[HALO + rows :] = jnp.where(odd, odd_ref[...], even_ref[...])

    def packed_start(first):
        return rows_s[first : first + PACK].reshape(PACK * chans, depth).T

    def left_side(pair, value, turned, low):
        group = lane_groups(value.shape, chans)
        own = (group >= 2 * pair) & (group < 2 * pair + 4)
        return jnp.concatenate([jnp.where(own, value, turned).astype(BF16), low], 1)

    def pieces(count):
        return [(first, min(first + PIECE, count)) for first in range(0, count, PIECE)]

    def to_points(row, field, behind):
        for first, last in reversed(pieces(groups)):
            fours = field(first, last)
            for point, form in enumerate(column_points(fours, behind)):
                high, low = split(form.reshape((last - first) * states, hid))
                points_s[point, row, first * states : last * states, :hid] = high
                points_s[point, row, first * states : last * states, hid:] = low
            behind = fours

    def second_hidden(chosen, row_first, col_first, beside=()):
        beside = list(beside)
        step = len(chosen)
        sums = []
        for point in range(6):
            left = jnp.concatenate(
                [
                    jnp.concatenate([points_s[point, i + a] for i in chosen], 0)
                    for a in range(3)
                ],
                1,
            )
            both = jnp.dot(left, wm_ref[point], preferred_element_type=F32)
            sums.append(both.reshape(step, groups, states, 2 * hid))
            if beside:
                beside.pop(0)()
        for r, i in enumerate(chosen):
            ok = in_field(row0 + row_first + i)
            for first, last in pieces(groups):
                parts = [m[r, first:last] for m in sums]
                parts = [m[:, :, :hid] + m[:, :, hid:] for m in parts]
                size = 4 * (last - first)
                field = jnp.stack(column_outputs(*parts), 1).reshape(size, states, hid)
                bias = mid_bias[ok, col_first + 4 * first : col_first + 4 * last]
                high, low = split(silu_of_double(field + bias).reshape(size * states, hid))
                place = slice(4 * first * states, 4 * last * states)
                hid2_s[i, place, :hid] = high
                hid2_s[i, place, hid:] = low

    def unit_taps(first, count):
        units = range(first, first + count)
        left = jnp.concatenate(
            [jnp.concatenate([hid2_s[2 * u + k] for u in units], 0) for k in range(4)], 1
        )
        taps = jnp.dot(left, wo_ref[...], preferred_element_type=F32)
        taps = taps.reshape(count, wide, states, 2 * hid)
        return [taps[u] for u in range(count)]

    def noise(taps, width, use):
        def work(first, last):
            size = last - first
            shape = (size, states, hid)
            group = lane_groups(shape, 2 * chans)
            one = []
            for unit in taps:
                both = unit[first : last + 2]
                both = both[:, :, :hid] + both[:, :, hid:]
                rest = jnp.where(group == 2, both[2:], both[:size])
                one.append(jnp.where(group == 1, both[1 : size + 1], rest))

            def turn(value, shift):
                return pltpu.roll(value.reshape(size * states, hid), shift, 1).reshape(shape)

            lower, even = group < 2, group % 2 == 0
            u0, u1, u2, u3 = one
            v0 = jnp.where(lower, u0, u2) + turn(jnp.where(lower, u2, u0), hid // 2)
            v1 = jnp.where(lower, u1, u3) + turn(jnp.where(lower, u3, u1), hid // 2)
            other = jnp.where(even, v1, v0)
            other = jnp.where(even, turn(other, hid - 2 * chans), turn(other, 2 * chans))
            use(first, last, jnp.where(even, v0, v1) + other + out_bias)

        for first in range(0, width, FEW):
            work(first, min(first + FEW, width))

    state = lax.broadcasted_iota(jnp.int32, (1, states, hid), 1)

    def earlier(value):
        value = jnp.where(state >= 1, pltpu.roll(value, 1, 1), 0.0)
        reach = 1
        while reach < states:
            value = value + jnp.where(state >= reach, pltpu.roll(value, reach, 1), 0.0)
            reach *= 2
        return value

    packs = start_s.shape[0]
    for p in range(packs):
        start_s[p] = packed_start(NET * p)

    near = wide + 8
    for pair in range(NET // 2):
        left = []
        for p in range(packs):
            value = start_s[p, :near]
            left.append(left_side(pair, value, pltpu.roll(value, hid // 2, 1), split(value)[1]))
        taps = jnp.dot(jnp.concatenate(left, 0), wi_ref[pair], preferred_element_type=F32)
        for p in range(packs):
            for r in range(2):
                t0, t1, t2 = (
                    taps[p * near : (p + 1) * near, (3 * r + k) * hid : (3 * r + k + 1) * hid]
                    for k in range(3)
                )
                common_s[NET * p + 2 * pair + r] = (
                    t0 + pltpu.roll(t1, near - 1, 0) + pltpu.roll(t2, near - 2, 0)
                )

    def first_points(i):
        ok = in_field(row0 - 5 + i)

        def field(first, last):
            place = slice(4 * first, 4 * last)
            value = silu_of_double(common_s[i, place][:, None, :] + in_bias[ok, place])
            return value.reshape(last - first, 4, states, hid)

        to_points(i, field, field(groups, groups + 1))

    packs = inputs_s.shape[0]
    for p in range(packs):
        start_s[p] = packed_start(REACH + NET * p)
        inputs_s[p, reach_cols * states :] = jnp.zeros(((wide - reach_cols) * states, hid), F32)
    group = lane_groups((1, hid), chans)

    def next_inputs(p, first, last, value):
        start = start_s[p, REACH + first : REACH + last]
        start = jnp.broadcast_to(start[:, None, :], (last - first, states, hid))
        row = group + (row0 - REACH + NET * p)
        keep = jnp.where((row >= 0) & (row < all_rows), 1.0, 0.0)
        drift = drift_x[None] * start + eps_s[first:last] * (value * keep)
        total = start + earlier(drift)
        inputs_s[p, first * states : last * states] = total.reshape((last - first) * states, hid)

    none = jnp.zeros((1, 4, states, hid), F32)

    def next_points(p):
        behind = none
        for first, last in reversed(pieces(groups)):
            size = (last - first) * states
            fours = inputs_s[p, 4 * first * states : 4 * last * states]
            fours = fours.reshape(last - first, 4, states, hid)
            place = slice((p * groups + first) * states, (p * groups + last) * states)
            for point, form in enumerate(column_points(fours, behind)):
                value = form.reshape(size, hid)
                parts_s[point, place] = value
                turned_s[point, place] = pltpu.roll(value, hid // 2, 1)
                low_s[point, place] = split(value)[1]
            behind = fours

    def second_rows(p, pair):
        own = slice(p * groups * states, (p + 1) * groups * states)
        products = []
        for point in range(6):
            left = left_side(pair, parts_s[point, own], turned_s[point, own], low_s[point, own])
            both = jnp.dot(left, wi_forms[pair, point], preferred_element_type=F32)
            products.append(both.reshape(groups, states, 2 * hid))
        for r in range(2):
            i = NET * p + 2 * pair + r
            ok = in_field(row0 - 2 + i)

            def field(first, last, r=r, ok=ok):
                parts = [m[first:last, :, r * hid : (r + 1) * hid] for m in products]
                value = jnp.stack(column_outputs(*parts), 1)
                bias = in_bias[ok, 3 + 4 * first : 3 + 4 * last].reshape(value.shape)
                return silu_of_double(value + bias)

            to_points(i, field, none)

    def last_drifts(first, last, value):
        size = (last - first) * states
        place = slice((REACH + first) * states, (REACH + last) * states)
        inputs = jnp.where(
            lane_groups((size, hid), chans) < PACK - REACH,
            pltpu.roll(inputs_s[0, place], hid - REACH * chans, 1),
            pltpu.roll(inputs_s[1, place], (NET - REACH) * chans, 1),
        ).reshape(value.shape)
        drift = drift_x[None] * inputs + drift_eps[None] * value
        last_s[first * states : last * states] = drift.reshape(size, hid)

    step = 4
    calls = [functools.partial(first_points, i) for i in range(rows + 10)]
    for call in calls[: step + 2]:
        call()
    taps, packs_ready = [], 0

    def second_inputs():
        p = packs_ready
        first = NET // 2 * p
        noise(taps[first : first + 4], reach_cols, functools.partial(next_inputs, p))
        next_points(p)
        for pair in range(NET // 2):
            second_rows(p, pair)

    for first in range(0, rows + 8, step):
        ahead = first + step + 2
        second_hidden(range(first, first + step), -4, 0, calls[ahead : ahead + step])
        if len(taps) >= NET // 2 * packs_ready + 4:
            second_inputs()
            packs_ready += 1
        taps += unit_taps(len(taps), (first + step - 2) // 2 - len(taps))
    second_hidden(range(step), -1, 3)
    second_inputs()
    taps = unit_taps(0, 1)
    second_hidden(range(step, rows + 2), -1, 3)
    taps += unit_taps(1, 3)
    noise(taps, cols, last_drifts)
    high, low = split(last_s[...].T)
    total = jnp.dot(high, sums_ref[...], preferred_element_type=F32) + jnp.dot(
        low, sums_ref[...], preferred_element_type=F32
    )
    start = mid_ref[...].reshape(rows * chans, depth)[:, HALO : HALO + cols]
    start = jnp.concatenate([start] * here, 1)
    width = here * cols
    for k in range(tm):
        value = start + total[:, k * width : (k + 1) * width]
        for r in range(rows):
            chunk_s[k, :, r, :] = value[r * chans : (r + 1) * chans]
    for k in range(tm):
        outs[k][...] = chunk_s[my_tm ^ k]


def join_kernel(tm, *refs):
    blocks, out_ref, held = refs[:tm], refs[tm], refs[tm + 1]
    here = out_ref.shape[0]
    cols = out_ref.shape[3] // tm
    for k in range(tm):
        held[k] = blocks[k][...]
    my_tm = lax.axis_index("tm")
    for k in range(tm):
        block = held[my_tm ^ k]
        for t in range(here):
            out_ref[t, :, :, k * cols : (k + 1) * cols] = block[:, :, t * cols : (t + 1) * cols]


def kernel_call(body, out_shape, in_specs, scratch=(), flops=0, read=0):
    vmem = pl.BlockSpec(memory_space=pltpu.VMEM)
    if isinstance(in_specs, int):
        in_specs = [vmem] * in_specs
    return pl.pallas_call(
        body,
        out_shape=out_shape,
        in_specs=in_specs,
        out_specs=jax.tree.map(lambda _: vmem, out_shape),
        scratch_shapes=list(scratch),
        compiler_params=pltpu.CompilerParams(vmem_limit_bytes=VMEM_LIMIT),
        cost_estimate=pl.CostEstimate(flops=flops, bytes_accessed=read, transcendentals=0),
    )


def in_hbm(value):
    return pltpu.with_memory_space_constraint(value, pltpu.HBM)


def on_device(start_latent, time_embed, drift_x, drift_eps, w_in, b_in, w_mid, b_mid, w_out, b_out):
    tm, space = lax.axis_size("tm"), lax.axis_size("space")
    chans, rows, all_cols = start_latent.shape
    here, hid = time_embed.shape
    states, cols = here * tm, all_cols // tm
    depth = -(-(cols + 2 * HALO) // 128) * 128
    assert rows == PACK and hid == PACK * chans
    shape, local = jax.ShapeDtypeStruct, pltpu.VMEM
    hbm = pl.BlockSpec(memory_space=pltpu.HBM)

    edge = local((HALO, chans, depth), F32)
    mid, even, odd, par = kernel_call(
        pack_kernel,
        (local((rows, chans, depth), F32), edge, edge, local((here, 2 * hid), F32)),
        [hbm] * 4,
        scratch=(
            pltpu.VMEM((chans, rows, all_cols), F32),
            pltpu.VMEM((here, hid), F32),
            pltpu.SMEM((here,), F32),
            pltpu.SMEM((here,), F32),
            pltpu.SemaphoreType.DMA((4,)),
        ),
        read=10**6,
    )(*map(in_hbm, (start_latent, time_embed, drift_x, drift_eps)))
    even = lax.ppermute(even, "space", [(i, i ^ 1) for i in range(space) if i ^ 1 < space])
    pairs = [(i, i + 1) for i in range(1, space - 1, 2)]
    odd = lax.ppermute(odd, "space", pairs + [(b, a) for a, b in pairs])
    pars = [par] + [
        lax.ppermute(par, "tm", [(i, i ^ k) for i in range(tm)]) for k in range(1, tm)
    ]

    weights = kernel_call(
        functools.partial(weights_kernel, states),
        (
            local((NET // 2, 2 * hid, 6 * hid), BF16),
            local((NET // 2, 6, 2 * hid, 2 * hid), BF16),
            local((6, 6 * hid, 2 * hid), BF16),
            local((8 * hid, 2 * hid), BF16),
            local((8, hid), F32),
            local((cols * states, cols * states), BF16),
        ),
        [hbm] * 6,
        scratch=(
            pltpu.VMEM((3, 3, chans, hid), F32),
            pltpu.VMEM((3, 3, hid, hid), F32),
            pltpu.VMEM((3, 3, chans, hid), F32),
            pltpu.VMEM((hid,), F32),
            pltpu.VMEM((hid,), F32),
            pltpu.VMEM((chans,), F32),
            pltpu.SemaphoreType.DMA((6,)),
        ),
        flops=10**7,
        read=8 * 10**6,
    )(*map(in_hbm, (w_in.transpose(0, 1, 3, 2), w_mid, w_out, b_in, b_mid, b_out)))
    wi, wi_forms, wm, wo, bias, sums = weights

    groups = (cols + 8) // 4
    wide = 4 * groups
    width = here * cols
    parts = (rows + HALO - 2) // NET * groups * states
    chunks = kernel_call(
        functools.partial(main_kernel, tm),
        tuple(local((chans, rows, width), F32) for _ in range(tm)),
        9 + tm,
        scratch=(
            pltpu.VMEM((rows + 2 * HALO, chans, depth), F32),
            pltpu.VMEM((states, 2 * hid), F32),
            pltpu.VMEM((tm, here, 2 * hid), F32),
            pltpu.VMEM(((rows + 2 * HALO - 2) // NET, depth, hid), F32),
            pltpu.VMEM((rows + 10, wide + 8, hid), F32),
            pltpu.VMEM((6, rows + 10, groups * states, 2 * hid), BF16),
            pltpu.VMEM((rows + 8, wide * states, 2 * hid), BF16),
            pltpu.VMEM(((rows + HALO - 2) // NET, wide * states, hid), F32),
            pltpu.VMEM((tm, chans, rows, width), F32),
            pltpu.VMEM((2, wide + 4, states, hid), F32),
            pltpu.VMEM((2, wide + 3, states, hid), F32),
            pltpu.VMEM((cols + HALO, states, hid), F32),
            *(pltpu.VMEM((6, parts, hid), kind) for kind in (F32, F32, BF16)),
            pltpu.VMEM((cols * states, hid), F32),
        ),
        flops=10**10,
        read=8 * 10**6,
    )(mid, even, odd, *pars, bias, wi, wi_forms, wm, wo, sums)

    blocks = [chunks[0]] + [
        lax.ppermute(chunks[k], "tm", [(i, i ^ k) for i in range(tm)]) for k in range(1, tm)
    ]
    return kernel_call(
        functools.partial(join_kernel, tm),
        shape((here, chans, rows, all_cols), F32),
        tm,
        scratch=(pltpu.VMEM((tm, chans, rows, width), F32),),
        read=10**6,
    )(*blocks)


def solution(mesh):
    in_specs = (
        P("group", "space", None),
        P("tm", None),
        P("tm"),
        P("tm"),
        P(),
        P(),
        P(),
        P(),
        P(),
        P(),
    )
    out_specs = P("tm", "group", "space", None)
    return jax.shard_map(
        on_device, mesh=mesh, in_specs=in_specs, out_specs=out_specs, check_vma=False
    )
```
